256 devices in a mesh: frame: 8 (over y, x_hi), space: 32 (over x_lo, z, core).
Axes of the slice: x: 4 (x_hi: 2, x_lo: 2; x = x_hi * 2 + x_lo), y: 4, z: 8, core: 2. Of those that a mesh axis runs over, the one named last changes fastest.
Arguments:
- latent: bfloat16 [16, 2048, 1152], P('frame', 'space'), may hold values from -6 to 6
- modulation: float32 [6, 1152], replicated, may hold values from -4 to 4, as said below
- w_spatial: bfloat16 [1152, 3456], P('space'), may hold values from -0.1875 to 0.1875
- w_spatial_out: bfloat16 [1152, 1152], P('space'), may hold values from -0.1875 to 0.1875
- caption_states: bfloat16 [300, 1152], replicated, may hold values from -6 to 6
- w_text_kv: bfloat16 [1152, 2304], P(None, 'space'), may hold values from -0.1875 to 0.1875
- w_cross_q: bfloat16 [1152, 1152], P('space'), may hold values from -0.1875 to 0.1875
- text_len: int32 [1], replicated, may hold values from 61 to 300
- w_time: bfloat16 [1152, 3456], P('space'), may hold values from -0.1875 to 0.1875
- w_time_out: bfloat16 [1152, 1152], P('space'), may hold values from -0.1875 to 0.1875
Outputs:
- result: bfloat16 [16, 2048, 1152], P('frame', 'space')
The draws below stay inside these ranges and needn't reach their ends.
Inputs may be any that keep to these rules, and one draw needn't show every extreme that they name: `modulation`: rows 0 and 3 are shifts, rows 1 and 4 scales, rows 2 and 5 gates.
All inputs are finite; a program needn't handle non-finite values.
Results may differ from the reference program's by a relative error of at most 0.025.
Values may be sent and summed in bfloat16 or wider, within the bound.
A program may use at most 128 MiB of HBM per device.

```python
import math
import jax
import jax.numpy as jnp
from jax import lax

D = 1152
HEADS = 16
HD = 72
TEXT = 300
FRAMES = 16
PATCHES = 2048


def draw_modulation(key, part):
    key = jax.random.fold_in(key, 7)
    base = jnp.clip(jax.random.normal(key, (6, D), jnp.float32), -4.0, 4.0)
    factors = jnp.array([0.3, 0.5, 0.8, 0.3, 0.5, 0.8], jnp.float32)[:, None]
    drawn = base * factors
    return drawn


def block_levels(stream_key, extent, shards, least, largest):
    loudness = 1.0
    for dim, parts in shards:
        heights = jax.random.uniform(jax.random.fold_in(jax.random.fold_in(stream_key, 6), dim), (parts,), jnp.float32, least / len(shards), largest / len(shards))
        loudness = loudness * jnp.repeat(jnp.exp(heights), extent[dim] // parts).reshape((-1,) + (1,) * (len(extent) - 1 - dim))
    return loudness


def bell_draw(own_key, extent, deviation, reach, split=(), kind=jnp.bfloat16):
    entries = deviation * jax.random.normal(own_key, extent, jnp.float32)
    if split:
        entries = entries * block_levels(own_key, extent, split, -0.22, 0.18)
    return jnp.clip(entries, -reach, reach).astype(kind)


def setup_inputs(seed: int = 0) -> dict:
    key_of = jax.random.split(jax.random.key(seed), 11)
    return {
        "latent": bell_draw(key_of[0], (FRAMES, PATCHES, D), 1.0, 6.0, ((0, 8), (1, 32))),
        "modulation": draw_modulation(jax.random.fold_in(key_of[10], 71), 0),
        "w_spatial": bell_draw(key_of[2], (D, 3 * D), D ** -0.5, 0.1875, ((0, 32),)),
        "w_spatial_out": bell_draw(key_of[3], (D, D), D ** -0.5, 0.1875, ((0, 32),)),
        "caption_states": bell_draw(key_of[4], (TEXT, D), 1.0, 6.0),
        "w_text_kv": bell_draw(key_of[5], (D, 2 * D), D ** -0.5, 0.1875, ((1, 32),)),
        "w_cross_q": bell_draw(key_of[6], (D, D), D ** -0.5, 0.1875, ((0, 32),)),
        "text_len": jax.random.randint(key_of[7], (1,), TEXT // 5 + 1, TEXT + 1).astype(jnp.int32),
        "w_time": bell_draw(key_of[8], (D, 3 * D), D ** -0.5, 0.1875, ((0, 32),)),
        "w_time_out": bell_draw(key_of[9], (D, D), D ** -0.5, 0.1875, ((0, 32),)),
    }


def modulate(states, shift, gain):
    values = states.astype(jnp.float32)
    row_mean = lax.optimization_barrier(jnp.mean(values, axis=-1, keepdims=True))
    centred = values - row_mean
    variance = lax.optimization_barrier(jnp.mean(centred * centred, axis=-1, keepdims=True))
    return (centred * lax.rsqrt(variance + 1e-06) * (1.0 + gain) + shift).astype(jnp.bfloat16)

def attend(query_rows, key_rows, value_rows):
    scores = jnp.dot(query_rows, key_rows.T, preferred_element_type=jnp.float32) / math.sqrt(HD)
    highest = lax.optimization_barrier(jnp.max(scores, axis=-1, keepdims=True))
    expsum = jnp.exp(scores - highest)
    weights = (expsum / lax.optimization_barrier(jnp.sum(expsum, axis=-1, keepdims=True))).astype(jnp.bfloat16)
    return jnp.dot(weights, value_rows, preferred_element_type=jnp.float32).astype(jnp.bfloat16)

def cross_attend(query_rows, text_keys, text_values, valid):
    queries = query_rows.reshape(-1, HEADS, HD).astype(jnp.float32)
    scores = jnp.einsum('rhe,jhe->hrj', queries, text_keys.astype(jnp.float32)) / math.sqrt(HD)
    scores = jnp.where(valid[None, None, :], scores, -jnp.inf)
    highest = lax.optimization_barrier(jnp.max(scores, axis=-1, keepdims=True))
    expsum = jnp.exp(scores - highest)
    weights = (expsum / lax.optimization_barrier(jnp.sum(expsum, axis=-1, keepdims=True))).astype(jnp.bfloat16)
    mixed = jnp.einsum('hrj,jhe->rhe', weights.astype(jnp.float32), text_values.astype(jnp.float32))
    return mixed.astype(jnp.bfloat16).reshape(-1, D)

def spatial_item(query_key_value):
    return attend(query_key_value[0], query_key_value[1], query_key_value[2])

def reference(latent, modulation, w_spatial, w_spatial_out, caption_states, w_text_kv, w_cross_q, text_len, w_time, w_time_out):
    flat = latent.reshape(FRAMES * PATCHES, D)
    normed = modulate(flat, modulation[0], modulation[1])
    qkv_s = jnp.dot(normed, w_spatial, preferred_element_type=jnp.float32).astype(jnp.bfloat16)
    items = qkv_s.reshape(FRAMES, PATCHES, 3, HEADS, HD).transpose(0, 3, 2, 1, 4).reshape(FRAMES * HEADS, 3, PATCHES, HD)
    spatial_pass = lax.map(spatial_item, items)
    spatial_pass = spatial_pass.reshape(FRAMES, HEADS, PATCHES, HD).transpose(0, 2, 1, 3).reshape(FRAMES * PATCHES, D)
    spatial_term = jnp.dot(spatial_pass, w_spatial_out, preferred_element_type=jnp.float32)
    after_space = (flat.astype(jnp.float32) + modulation[2] * spatial_term).astype(jnp.bfloat16)
    text_kv = jnp.dot(caption_states, w_text_kv, preferred_element_type=jnp.float32).astype(jnp.bfloat16)
    text_keys = text_kv[:, :D].reshape(TEXT, HEADS, HD)
    text_values = text_kv[:, D:].reshape(TEXT, HEADS, HD)
    cross_q = jnp.dot(after_space, w_cross_q, preferred_element_type=jnp.float32).astype(jnp.bfloat16)
    valid = jnp.arange(TEXT) < text_len[0]

    def cross_frame(frame_rows):
        return cross_attend(frame_rows, text_keys, text_values, valid)
    crossed = lax.map(cross_frame, cross_q.reshape(FRAMES, PATCHES, D)).reshape(FRAMES * PATCHES, D)
    after_text = (after_space.astype(jnp.float32) + crossed.astype(jnp.float32)).astype(jnp.bfloat16)
    normed_t = modulate(after_text, modulation[3], modulation[4])
    qkv_t = jnp.dot(normed_t, w_time, preferred_element_type=jnp.float32).astype(jnp.bfloat16)
    qkv_t = qkv_t.reshape(FRAMES, PATCHES, 3, HEADS, HD)
    queries = qkv_t[:, :, 0].astype(jnp.float32)
    key_rows = qkv_t[:, :, 1].astype(jnp.float32)
    value_rows = qkv_t[:, :, 2].astype(jnp.float32)
    scores = jnp.einsum('fphe,gphe->phfg', queries, key_rows) / math.sqrt(HD)
    highest = lax.optimization_barrier(jnp.max(scores, axis=-1, keepdims=True))
    expsum = jnp.exp(scores - highest)
    weights = (expsum / lax.optimization_barrier(jnp.sum(expsum, axis=-1, keepdims=True))).astype(jnp.bfloat16)
    temporal = jnp.einsum('phfg,gphe->fphe', weights.astype(jnp.float32), value_rows).astype(jnp.bfloat16)
    temporal = temporal.reshape(FRAMES * PATCHES, D)
    time_term = jnp.dot(temporal, w_time_out, preferred_element_type=jnp.float32)
    result = (after_text.astype(jnp.float32) + modulation[5] * time_term).astype(jnp.bfloat16)
    return result.reshape(FRAMES, PATCHES, D)
```

```python
import math

import jax
import jax.numpy as jnp
from jax import lax
from jax.sharding import PartitionSpec as P

D = 1152
HEADS = 16
HD = 72


def modulate(states, shift, gain):
    values = states.astype(jnp.float32)
    row_mean = jnp.mean(values, axis=-1, keepdims=True)
    centred = values - row_mean
    variance = jnp.mean(centred * centred, axis=-1, keepdims=True)
    return (centred * lax.rsqrt(variance + 1e-06) * (1.0 + gain) + shift).astype(jnp.bfloat16)


def attend(query_rows, key_rows, value_rows):
    scores = jnp.dot(query_rows, key_rows.T, preferred_element_type=jnp.float32) / math.sqrt(HD)
    highest = jnp.max(scores, axis=-1, keepdims=True)
    expsum = jnp.exp(scores - highest)
    weights = (expsum / jnp.sum(expsum, axis=-1, keepdims=True)).astype(jnp.bfloat16)
    return jnp.dot(weights, value_rows, preferred_element_type=jnp.float32).astype(jnp.bfloat16)


def spatial_item(query_key_value):
    query_rows, key_rows, value_rows = query_key_value
    row_count = query_rows.shape[0]
    block_rows = min(512, row_count)
    block_list = query_rows.reshape(row_count // block_rows, block_rows, HD)

    def one_block(block):
        return attend(block, key_rows, value_rows)

    return lax.map(one_block, block_list).reshape(row_count, HD)


def project(rows, weight):
    return jnp.dot(rows, weight, preferred_element_type=jnp.float32)


def local(
    latent,
    modulation,
    w_spatial,
    w_spatial_out,
    caption_states,
    w_text_kv,
    w_cross_q,
    text_len,
    w_time,
    w_time_out,
):
    frame_rows, patch_rows = (latent.shape[0], latent.shape[1])
    tokens = frame_rows * patch_rows
    flat = latent.reshape(tokens, D)
    local_kv = jnp.dot(caption_states, w_text_kv, preferred_element_type=jnp.float32).astype(
        jnp.bfloat16
    )
    shard_rows = w_spatial.shape[0]
    text_flat = local_kv.reshape(shard_rows, -1)
    joined = jnp.concatenate(
        [w_spatial, w_spatial_out, w_cross_q, w_time, w_time_out, text_flat], axis=1
    )
    joined = lax.all_gather(joined, "space", axis=0, tiled=True)
    w_spatial = joined[:, : 3 * D]
    w_spatial_out = joined[:, 3 * D : 4 * D]
    w_cross_q = joined[:, 4 * D : 5 * D]
    w_time = joined[:, 5 * D : 8 * D]
    w_time_out = joined[:, 8 * D : 9 * D]
    text_kv = joined[:, 9 * D :].reshape(-1, caption_states.shape[0], local_kv.shape[1])
    text_kv = text_kv.transpose(1, 0, 2).reshape(caption_states.shape[0], 2 * D)
    normed = modulate(flat, modulation[0], modulation[1])
    qkv_s = project(normed, w_spatial).astype(jnp.bfloat16)
    sectioned = qkv_s.reshape(frame_rows, patch_rows, 3, HEADS, HD).transpose(2, 0, 3, 1, 4)
    sectioned = sectioned.reshape(3, frame_rows * HEADS, patch_rows * HD)
    moved = lax.all_to_all(sectioned, "space", split_axis=1, concat_axis=2, tiled=True)
    item_count = moved.shape[1]
    moved = moved.reshape(3, item_count, -1, HD)
    spatial_pass = lax.map(spatial_item, (moved[0], moved[1], moved[2]))
    returned = lax.all_to_all(
        spatial_pass.reshape(item_count, -1), "space", split_axis=1, concat_axis=0, tiled=True
    )
    spatial_rows = (
        returned.reshape(frame_rows, HEADS, patch_rows, HD).transpose(0, 2, 1, 3).reshape(tokens, D)
    )
    spatial_term = project(spatial_rows, w_spatial_out)
    after_space = (flat.astype(jnp.float32) + modulation[2] * spatial_term).astype(jnp.bfloat16)
    text_count = text_kv.shape[0]
    text_keys = text_kv[:, :D].reshape(text_count, HEADS, HD)
    text_values = text_kv[:, D:].reshape(text_count, HEADS, HD)
    cross_q = project(after_space, w_cross_q).astype(jnp.bfloat16).reshape(tokens, HEADS, HD)
    valid = jnp.arange(text_count) < text_len[0]
    scores = jnp.einsum(
        "rhe,jhe->hrj", cross_q, text_keys, preferred_element_type=jnp.float32
    ) / math.sqrt(HD)
    scores = jnp.where(valid[None, None, :], scores, -jnp.inf)
    highest = jnp.max(scores, axis=-1, keepdims=True)
    expsum = jnp.exp(scores - highest)
    weights = (expsum / jnp.sum(expsum, axis=-1, keepdims=True)).astype(jnp.bfloat16)
    crossed = jnp.einsum("hrj,jhe->rhe", weights, text_values, preferred_element_type=jnp.float32)
    crossed = crossed.astype(jnp.bfloat16).reshape(tokens, D)
    after_text = (after_space.astype(jnp.float32) + crossed.astype(jnp.float32)).astype(
        jnp.bfloat16
    )
    normed_t = modulate(after_text, modulation[3], modulation[4])
    qkv_t = project(normed_t, w_time).astype(jnp.bfloat16)
    sectioned_t = qkv_t.reshape(frame_rows, patch_rows, 3, HEADS, HD).transpose(2, 1, 3, 0, 4)
    sectioned_t = sectioned_t.reshape(3, patch_rows * HEADS, frame_rows * HD)
    moved_transposed = lax.all_to_all(sectioned_t, "frame", split_axis=1, concat_axis=2, tiled=True)
    time_items = moved_transposed.shape[1]
    moved_transposed = moved_transposed.reshape(3, time_items, -1, HD)
    time_scores = jnp.einsum(
        "iou,icu->ioc", moved_transposed[0], moved_transposed[1], preferred_element_type=jnp.float32
    ) / math.sqrt(HD)
    temporal_upper = jnp.max(time_scores, axis=-1, keepdims=True)
    time_exp = jnp.exp(time_scores - temporal_upper)
    temporal_weights = (time_exp / jnp.sum(time_exp, axis=-1, keepdims=True)).astype(jnp.bfloat16)
    temporal = jnp.einsum(
        "lmo,log->lmg", temporal_weights, moved_transposed[2], preferred_element_type=jnp.float32
    )
    temporal = temporal.astype(jnp.bfloat16).reshape(time_items, -1)
    back_t = lax.all_to_all(temporal, "frame", split_axis=1, concat_axis=0, tiled=True)
    temporal_rows = (
        back_t.reshape(patch_rows, HEADS, frame_rows, HD).transpose(2, 0, 1, 3).reshape(tokens, D)
    )
    time_term = project(temporal_rows, w_time_out)
    result = (after_text.astype(jnp.float32) + modulation[5] * time_term).astype(jnp.bfloat16)
    return result.reshape(frame_rows, patch_rows, D)


def solution(mesh):
    placed = (
        P("frame", "space", None),
        P(),
        P("space", None),
        P("space", None),
        P(),
        P(None, "space"),
        P("space", None),
        P(),
        P("space", None),
        P("space", None),
    )
    return jax.shard_map(
        local, mesh=mesh, in_specs=placed, out_specs=P("frame", "space", None), check_vma=False
    )
```

```python
import functools
import math

import jax
import jax.numpy as jnp
from jax import lax
from jax.experimental import pallas as pl
from jax.experimental.pallas import tpu as pltpu
from jax.sharding import PartitionSpec as P

D = 1152
HEADS = 16
HD = 72
ROWS = 36
HALF = 576
TROWS = 40
TEXT = 8 * TROWS
CA = 384
CB = 512
MESH = pl.DeviceIdType.MESH
BF = jnp.bfloat16
F32 = jnp.float32
SCALE = 1.0 / math.sqrt(HD)
LOG2E = 1.4426950408889634
NSEM = 256


def modulate(values, shift, gain):
    row_mean = jnp.mean(values, axis=-1, keepdims=True)
    centred = values - row_mean
    variance = jnp.mean(centred * centred, axis=-1, keepdims=True)
    return (centred * lax.rsqrt(variance + 1e-06) * (1.0 + gain) + shift).astype(BF)


def nt(left, right):
    return lax.dot_general(left, right, (((1,), (1,)), ((), ())), preferred_element_type=F32)


def mm(left, right):
    return jnp.dot(left, right, preferred_element_type=F32)


def where_tile(tile):
    if tile < 16:
        return 0, tile // 2, 128 * (tile % 2)
    if tile < 24:
        return 0, tile - 16, 256
    return 1, (tile - 24) // 4, 128 * ((tile - 24) % 4)


def runs(first, count):
    found = []
    for tile in range(first, first + count):
        buf, part, col = where_tile(tile)
        if found:
            at, b, p, c, w = found[-1]
            if (b, p, c + w) == (buf, part, col):
                found[-1] = (at, b, p, c, w + 128)
                continue
        found.append((128 * (tile - first), buf, part, col, 128))
    return found


def kernel(
    latent, mod, wsp, wa, wb, tx, bias, out,
    nb, tok, res, s0, wqk, wvt, qb, kb, vt, scores, ot, oi,
    za, zb, ga, gb, gt, acc, xb, qt, at, ar, rs, rr, ssem, rsem,
):
    fr = lax.axis_index("frame")
    sp = lax.axis_index("space")
    y, xh = fr // 2, fr % 2
    xl, z, c = sp // 16, (sp // 2) % 8, sp % 2
    x = 2 * xh + xl
    oc = 1 - c

    def dev(y_, x_, z_, c_):
        return (y_ * 2 + x_ // 2, (x_ % 2) * 16 + z_ * 2 + c_)

    partner = dev(y, x, z, oc)
    zn = [dev(y, x, (z + 1) % 8, c), dev(y, x, (z + 7) % 8, c)]
    xn = [dev(y, (x + 1) % 4, z, c), dev(y, (x + 3) % 4, z, c)]
    xmate = dev(y, 2 * xh + (1 - xl), z, c)
    yn = [dev((y + d) % 4, x, z, c) for d in (1, 3, 2)]

    ids = [0]
    started = []

    def reserve(n):
        first = ids[0]
        ids[0] += n
        return first

    def send(src, dst, target):
        i = reserve(1)
        copy = pltpu.make_async_remote_copy(
            src_ref=src, dst_ref=dst, send_sem=ssem.at[i], recv_sem=rsem.at[i],
            device_id=target, device_id_type=MESH,
        )
        copy.start()
        started.append(copy)
        return copy

    barrier = pltpu.get_barrier_semaphore()
    for i in range(1, 32):
        pl.semaphore_signal(barrier, inc=1, device_id=(fr, (sp + i) % 32), device_id_type=MESH)
    for i in range(1, 8):
        for core in range(2):
            pl.semaphore_signal(
                barrier, inc=1, device_id=((fr + i) % 8, xl * 16 + z * 2 + core), device_id_type=MESH
            )
    pl.semaphore_signal(
        barrier, inc=1, device_id=dev(y, 2 * (1 - xh) + (1 - xl), z, c), device_id_type=MESH
    )

    for i in range(2):
        nb[i] = modulate(latent[i].astype(F32), mod[0:1], mod[1:2])
    tok[z, xl, c] = nb[xl]
    res[c] = latent[c]
    za[z, c] = wa[c]
    zb[z, c] = wb[c]
    part = 2 * y + c
    gt[part, xl, z, c] = tx[c]
    s0[xl, z, c] = wsp[2 * z + c]
    pl.semaphore_wait(barrier, 46)

    init_a = send(wa.at[oc], za.at[z, c], partner)
    init_t = send(tx.at[oc], gt.at[2 * y + oc, xl, z, c], partner)
    s_in = [send(wsp.at[2 * z + oc], s0.at[xl, z, c], partner)]
    tok_x = send(nb.at[1 - xl], tok.at[z, xl, c], xmate)
    init_b = send(wb.at[oc], zb.at[z, c], partner)
    res_in = send(latent.at[oc], res.at[c], partner)
    for d in (1, 7, 2, 6, 3, 5, 4):
        zt = (z + d) % 8
        s_in.append(send(wsp.at[2 * zt + c], s0.at[xl, z, c], dev(y, x, zt, c)))
        s_in.append(send(wsp.at[2 * zt + oc], s0.at[xl, z, c], dev(y, x, zt, oc)))

    def block(step, way):
        return (z + (8 - step if way == 0 else step)) % 8

    class Ring:
        def __init__(self, whole, halves):
            self.whole, self.halves, self.copies = whole, halves, {}

        def go(self, step):
            for way in range(2):
                b = block(step, way)
                ref = self.whole(b) if step < 3 else self.halves(b, way)
                self.copies[step, way] = send(ref, ref, zn[way])

        def come(self, step):
            for way in range(2):
                self.copies[step - 1, way].wait_recv()

    ring_a = Ring(lambda b: za.at[b], lambda b, h: za.at[b, h])
    ring_b = Ring(lambda b: zb.at[b], lambda b, h: zb.at[b, h])
    ring_t = Ring(lambda b: gt.at[part, xl, b], lambda b, h: gt.at[part, xl, b, h])
    ring_0 = Ring(lambda b: tok.at[b, xl, c], None)
    ring_1 = Ring(lambda b: tok.at[b, 1 - xl, c], None)
    tok_core = {}

    def tok_ring(ring, sub, step):
        if step < 3:
            ring.go(step)
        else:
            b = block(3, 0 if sub == 0 else 1)
            way = 0 if sub == 0 else 1
            ref = tok.at[b, xl if sub == 0 else 1 - xl, c]
            ring.copies[3, way] = send(ref, ref, zn[way])

    def tok_share(b, lo, key):
        ref = tok.at[b, lo, c]
        tok_core[key] = send(ref, ref, partner)

    init_a.wait_recv()
    ring_a.go(0)
    ring_0.go(0)
    tok_share(z, xl, (0, 0, 0))
    init_t.wait_recv()
    ring_t.go(0)
    tok_x.wait_recv()
    ring_1.go(0)
    tok_share(z, 1 - xl, (0, 0, 1))
    init_b.wait_recv()
    ring_b.go(0)

    def tok_step(step):
        for way in range(2):
            for sub, ring in ((0, ring_0), (1, ring_1)):
                ring.copies[step - 1, way].wait_recv()
        if step < 4:
            tok_ring(ring_0, 0, step)
            tok_ring(ring_1, 1, step)
        for way in range(2):
            for sub in range(2):
                tok_share(block(step, way), xl if sub == 0 else 1 - xl, (step, way, sub))

    def tok_last():
        ring_0.copies[3, 0].wait_recv()
        ring_1.copies[3, 1].wait_recv()
        tok_share(block(4, 0), xl, (4, 0, 0))
        tok_share(block(4, 0), 1 - xl, (4, 0, 1))

    def tok_ready(step, way):
        for sub in range(2):
            tok_core[step, way, sub].wait_recv()

    class Spread:
        def __init__(self, lo_rows, half_rows, first, second):
            self.lo_rows, self.half_rows = lo_rows, half_rows
            self.x_copies, self.core_copies = [], []

        def start(self):
            mine = self.lo_rows(part, xl)
            self.y_copies = [send(mine, mine, t) for t in yn]
            self.spread(y)

        def spread(self, yq):
            e = 2 * yq + c
            xs = []
            for way in range(2):
                ref = self.half_rows(e, xl, way)
                xs.append(send(ref, ref, xn[way]))
            self.x_copies.append((e, xs))
            ref = self.lo_rows(e, xl)
            self.core_copies.append(send(ref, ref, partner))

        def y_come(self, k):
            self.y_copies[k].wait_recv()
            self.spread((y + 4 - (1, 3, 2)[k]) % 4)

        def x_come(self, k):
            e, xs = self.x_copies[k]
            for way in range(2):
                xs[way].wait_recv()
                ref = self.half_rows(e, 1 - xl, way)
                self.core_copies.append(send(ref, ref, partner))

        def finish(self):
            for copy in self.core_copies:
                copy.wait_recv()

    def rows_of(buf):
        def lo_rows(e, lo):
            return buf.at[e, pl.ds(pl.multiple_of(lo * HALF, HALF), HALF)]

        def half_rows(e, lo, way):
            return buf.at[e, pl.ds(pl.multiple_of(lo * HALF + way * (HALF // 2), HALF // 2), HALF // 2)]

        return lo_rows, half_rows

    spread_a = Spread(*rows_of(ga), 0, 0)
    spread_b = Spread(*rows_of(gb), 0, 0)
    spread_t = Spread(
        lambda e, lo: gt.at[e, lo], lambda e, lo, way: gt.at[e, lo, pl.ds(4 * way, 4)], 0, 0
    )

    def compact(zref, gref):
        for k in range(4):
            rows = jnp.concatenate([zref[2 * k + i // 2, i % 2] for i in range(4)], axis=0)
            gref[part, pl.ds(pl.multiple_of(xl * HALF + 144 * k, 144), 144)] = rows

    def qkv(b):
        rows = tok[b].reshape(256, D)
        qk = mm(rows, wqk[...]).astype(BF)
        qb[b] = qk[:, :128]
        kb[b] = qk[:, 128:]
        v = nt(wvt[...], rows)
        ones = lax.broadcasted_iota(jnp.int32, v.shape, 0) == HD
        vt[b] = jnp.where(ones, 1.0, v).astype(BF)

    for step in (1, 2):
        ring_a.come(step)
        ring_a.go(step)
        ring_t.come(step)
        ring_t.go(step)
    for copy in s_in:
        copy.wait_recv()
    s_x = [
        send(s0.at[xl, pl.ds(4 * way, 4)], s0.at[xl, pl.ds(4 * way, 4)], xn[way]) for way in range(2)
    ]
    tok_step(1)
    ring_b.come(1)
    ring_b.go(1)
    ring_a.come(3)
    ring_a.go(3)
    ring_t.come(3)
    ring_t.go(3)
    for copy in s_x:
        copy.wait_recv()
    joined = s0[...].reshape(32 * ROWS, 256).astype(F32)
    blank = jnp.zeros((D, 128 - HD), F32)
    wqk[...] = jnp.concatenate([joined[:, :HD], blank, joined[:, HD : 2 * HD], blank], axis=1).astype(BF)
    wvt[...] = jnp.concatenate([joined[:, 2 * HD : 3 * HD], blank], axis=1).T[:80].astype(BF)
    ring_a.come(4)
    compact(za, ga)
    spread_a.start()
    ring_t.come(4)
    spread_t.start()
    tok_ready(0, 0)
    qkv(z)
    ring_b.come(2)
    ring_b.go(2)
    tok_step(2)
    for way in range(2):
        tok_ready(1, way)
        qkv(block(1, way))
    ring_b.come(3)
    ring_b.go(3)
    spread_a.y_come(0)
    spread_a.y_come(1)
    tok_step(3)
    ring_b.come(4)
    compact(zb, gb)
    spread_b.start()
    for way in range(2):
        tok_ready(2, way)
        qkv(block(2, way))
    spread_t.y_come(0)
    spread_t.y_come(1)
    spread_a.y_come(2)
    spread_a.x_come(0)
    spread_t.y_come(2)
    spread_t.x_come(0)
    tok_last()
    for way in range(2):
        tok_ready(3, way)
        qkv(block(3, way))
    tok_ready(4, 0)
    qkv(block(4, 0))

    oi_id = reserve(16)
    head = 2 * z + c

    def attn_copy(i, lo):
        zt = (z + 1 + i) % 8
        i_send = oi_id + 2 * i + lo
        return (
            pltpu.make_async_remote_copy(
                src_ref=ot.at[zt, lo], dst_ref=oi.at[head],
                send_sem=ssem.at[i_send], recv_sem=rsem.at[oi_id + head],
                device_id=(fr, lo * 16 + zt * 2 + xl), device_id_type=MESH,
            ),
            pltpu.make_async_copy(ot.at[zt, lo], oi.at[head], rsem.at[oi_id + head]),
            jnp.logical_and(zt == z, jnp.logical_and(xl == lo, c == xl)),
        )

    def tile(i, carry):
        zt = (z + 1 + i) % 8
        queries = qb[zt]
        top = jnp.full((1, 256), -jnp.inf, F32)
        for k in range(4):
            s = nt(kb[2 * k : 2 * k + 2].reshape(512, 128), queries)
            scores[512 * k : 512 * (k + 1)] = s
            top = jnp.maximum(top, jnp.max(s, axis=0, keepdims=True))
        top = top * (SCALE * LOG2E)
        total = jnp.zeros((80, 256), F32)
        for k in range(8):
            p = jnp.exp2(scores[256 * k : 256 * (k + 1)] * (SCALE * LOG2E) - top)
            total = total + mm(vt[k], p.astype(BF))
        mixed = (total[:HD] / total[HD : HD + 1]).astype(BF)
        for lo in range(2):
            ot[zt, lo] = mixed[:, 128 * lo : 128 * (lo + 1)]
            far, near, own = attn_copy(i, lo)

            @pl.when(own)
            def _():
                near.start()

            @pl.when(jnp.logical_not(own))
            def _():
                far.start()

        return carry

    lax.fori_loop(0, 4, tile, 0)
    spread_b.y_come(0)
    spread_b.y_come(1)
    spread_a.x_come(1)
    spread_a.x_come(2)
    spread_t.x_come(1)
    spread_t.x_come(2)
    lax.fori_loop(4, 8, tile, 0)
    spread_a.x_come(3)
    spread_t.x_come(3)
    spread_b.x_come(0)
    for i in range(HEADS):
        pltpu.make_async_copy(ot.at[0, 0], oi.at[i], rsem.at[oi_id + i]).wait()

    bufs = (ga, gb)

    def project(rows, first, count, put):
        for at_col, buf, e, col, width in runs(first, count):
            put(at_col, width, mm(rows, bufs[buf][e, :, col : col + width]))

    def put_acc(at_col, width, value):
        acc[:, at_col : at_col + width] = value

    spread_a.finish()
    rows = oi[...].reshape(D, 128).T
    project(rows, 0, 9, put_acc)
    res_in.wait_recv()
    own = res[...].reshape(128, D).astype(F32)
    after_space = (own + mod[2:3] * acc[...]).astype(BF)

    def put_qt(at_col, width, value):
        qt[:, at_col : at_col + width] = value.astype(BF)

    project(after_space, 9, 9, put_qt)
    qt[:, D : D + 128] = jnp.zeros((128, 128), BF)
    spread_b.y_come(2)
    spread_b.x_come(1)
    spread_t.finish()
    mixed = []
    for h in range(HEADS):
        keys = gt[:, 0, h // 2, h % 2].reshape(TEXT, 128)
        values = gt[:, 1, h // 2, h % 2].reshape(TEXT, 128)
        s = nt(qt[:, HD * h : HD * h + 128], keys) * SCALE + bias[...]
        p = jnp.exp(s - jnp.max(s, axis=-1, keepdims=True))
        w = (p / jnp.sum(p, axis=-1, keepdims=True)).astype(BF)
        mixed.append(mm(w, values)[:, :HD])
    crossed = jnp.concatenate(mixed, axis=1).astype(BF)
    after_text = (after_space.astype(F32) + crossed.astype(F32)).astype(BF)
    at[...] = after_text.reshape(16, 8, D)

    me = 2 * fr + c
    ar[me] = at[me]
    time_in = []
    for k in range(1, 16):
        p = (me + k) % 16
        time_in.append(send(at.at[p], ar.at[me], (p // 2, xl * 16 + z * 2 + p % 2)))
    spread_b.x_come(2)
    for copy in time_in:
        copy.wait_recv()
    tokens = ar[...].reshape(128, D).astype(F32)
    xb[...] = modulate(tokens, mod[3:4], mod[4:5])
    spread_b.x_come(3)
    spread_b.finish()
    project(xb[...], 18, 27, put_qt)
    qt[:, 3 * D :] = jnp.zeros((128, 128), BF)
    lanes = lax.broadcasted_iota(jnp.int32, (128, 128), 1)
    subs = lax.broadcasted_iota(jnp.int32, (128, 128), 0)
    same = (lanes % 8) == (subs % 8)
    real = lanes < HD
    mixed = []
    for h in range(HEADS):
        q = qt[:, HD * h : HD * h + 128]
        k = jnp.where(real, qt[:, D + HD * h : D + HD * h + 128], 0)
        v = qt[:, 2 * D + HD * h : 2 * D + HD * h + 128]
        s = jnp.where(same, nt(q, k) * SCALE, -jnp.inf)
        p = jnp.exp(s - jnp.max(s, axis=-1, keepdims=True))
        w = (p / jnp.sum(p, axis=-1, keepdims=True)).astype(BF)
        mixed.append(mm(w, v)[:, :HD])
    temporal = jnp.concatenate(mixed, axis=1).astype(BF)
    project(temporal, 45, 9, put_acc)
    result = (ar[...].reshape(128, D).astype(F32) + mod[5:6] * acc[...]).astype(BF)
    rs[...] = result.reshape(8, 2, 8, D)

    back_id = reserve(8)
    slot = (2 * fr + c) % 8
    back = []
    for k in range(8):
        ft = (fr + k) % 8
        far = pltpu.make_async_remote_copy(
            src_ref=rs.at[ft], dst_ref=rr.at[slot],
            send_sem=ssem.at[back_id + k], recv_sem=rsem.at[back_id + slot],
            device_id=(ft, xl * 16 + z * 2 + fr // 4), device_id_type=MESH,
        )
        back.append(far)
        if k == 0:
            near = pltpu.make_async_copy(rs.at[ft], rr.at[slot], rsem.at[back_id + slot])

            @pl.when(c == fr // 4)
            def _():
                near.start()

            @pl.when(c != fr // 4)
            def _():
                far.start()
        else:
            far.start()
    for k in range(8):
        pltpu.make_async_copy(rs.at[0], rr.at[k], rsem.at[back_id + k]).wait()
    for i in range(2):
        out[i] = rr[:, i].reshape(64, D)

    for copy in started:
        copy.wait_send()
    for i in range(8):
        for lo in range(2):
            far, near, own = attn_copy(i, lo)

            @pl.when(jnp.logical_not(own))
            def _():
                far.wait_send()

    @pl.when(c != fr // 4)
    def _():
        back[0].wait_send()

    for k in range(1, 8):
        back[k].wait_send()


def local(
    latent, modulation, w_spatial, w_spatial_out, caption_states, w_text_kv, w_cross_q, text_len,
    w_time, w_time_out,
):
    y = lax.axis_index("frame") // 2
    wsp = w_spatial.reshape(ROWS, 3, HEADS, HD).transpose(2, 0, 1, 3).reshape(HEADS, ROWS, 3 * HD)
    wsp = jnp.pad(wsp, ((0, 0), (0, 0), (0, 256 - 3 * HD)))
    joined = jnp.concatenate(
        [w_spatial_out, w_cross_q, w_time, w_time_out, jnp.zeros((ROWS, 256), BF)], axis=1
    )

    def cut(first, width):
        piece = lax.dynamic_slice(joined, (0, first + 2 * width * y), (ROWS, 2 * width))
        return piece.reshape(ROWS, 2, width).transpose(1, 0, 2)

    wa = jnp.concatenate([cut(0, 256), cut(2048, 128)], axis=2)
    wb = cut(3072, CB)
    text_count = caption_states.shape[0]
    caption = jnp.pad(caption_states, ((0, TEXT - text_count), (0, 0)))
    caption = lax.dynamic_slice(caption, (2 * TROWS * y, 0), (2 * TROWS, D))
    text = jnp.dot(caption, w_text_kv, preferred_element_type=F32).astype(BF)
    text = jnp.pad(text, ((0, 0), (0, 128 - HD))).reshape(2, TROWS, 128)
    bias = jnp.where(jnp.arange(TEXT) < text_len[0], 0.0, -jnp.inf).astype(F32)[None, :]

    vmem = pl.BlockSpec(memory_space=pltpu.VMEM)
    return pl.pallas_call(
        kernel,
        out_shape=jax.ShapeDtypeStruct(latent.shape, BF),
        in_specs=[vmem] * 7,
        out_specs=vmem,
        scratch_shapes=[
            pltpu.VMEM((2, 64, D), BF),
            pltpu.VMEM((8, 2, 2, 64, D), BF),
            pltpu.VMEM((2, 64, D), BF),
            pltpu.VMEM((2, 8, 2, ROWS, 256), BF),
            pltpu.VMEM((D, 256), BF),
            pltpu.VMEM((80, D), BF),
            pltpu.VMEM((8, 256, 128), BF),
            pltpu.VMEM((8, 256, 128), BF),
            pltpu.VMEM((8, 80, 256), BF),
            pltpu.VMEM((2048, 256), F32),
            pltpu.VMEM((8, 2, HD, 128), BF),
            pltpu.VMEM((HEADS, HD, 128), BF),
            pltpu.VMEM((8, 2, ROWS, CA), BF),
            pltpu.VMEM((8, 2, ROWS, CB), BF),
            pltpu.VMEM((8, D, CA), BF),
            pltpu.VMEM((8, D, CB), BF),
            pltpu.VMEM((8, 2, 8, 2, TROWS, 128), BF),
            pltpu.VMEM((128, D), F32),
            pltpu.VMEM((128, D), BF),
            pltpu.VMEM((128, 3 * D + 128), BF),
            pltpu.VMEM((16, 8, D), BF),
            pltpu.VMEM((16, 8, D), BF),
            pltpu.VMEM((8, 2, 8, D), BF),
            pltpu.VMEM((8, 2, 8, D), BF),
            pltpu.SemaphoreType.DMA((NSEM,)),
            pltpu.SemaphoreType.DMA((NSEM,)),
        ],
        compiler_params=pltpu.CompilerParams(
            collective_id=0, has_side_effects=True, vmem_limit_bytes=60 << 20
        ),
        name="block",
    )(latent, modulation, wsp, wa, wb, text, bias)


def solution(mesh):
    placed = (
        P("frame", "space", None),
        P(),
        P("space", None),
        P("space", None),
        P(),
        P(None, "space"),
        P("space", None),
        P(),
        P("space", None),
        P("space", None),
    )
    return jax.shard_map(
        local, mesh=mesh, in_specs=placed, out_specs=P("frame", "space", None), check_vma=False
    )
```

```python
import functools
import math

import jax
import jax.numpy as jnp
from jax import lax
from jax.experimental import pallas as pl
from jax.experimental.pallas import tpu as pltpu
from jax.sharding import PartitionSpec as P

D = 1152
HEADS = 16
HD = 72
ROWS = 36
HALF = 576
TROWS = 40
TEXT = 8 * TROWS
CA = 384
CB = 512
MESH = pl.DeviceIdType.MESH
BF = jnp.bfloat16
F32 = jnp.float32
SCALE = 1.0 / math.sqrt(HD)
LOG2E = 1.4426950408889634
NSEM = 256


def modulate(values, shift, gain):
    row_mean = jnp.mean(values, axis=-1, keepdims=True)
    centred = values - row_mean
    variance = jnp.mean(centred * centred, axis=-1, keepdims=True)
    return (centred * lax.rsqrt(variance + 1e-06) * (1.0 + gain) + shift).astype(BF)


def nt(left, right):
    return lax.dot_general(left, right, (((1,), (1,)), ((), ())), preferred_element_type=F32)


def mm(left, right):
    return jnp.dot(left, right, preferred_element_type=F32)


def where_tile(tile):
    if tile < 16:
        return 0, tile // 2, 128 * (tile % 2)
    if tile < 24:
        return 0, tile - 16, 256
    return 1, (tile - 24) // 4, 128 * ((tile - 24) % 4)


def runs(first, count):
    found = []
    for tile in range(first, first + count):
        buf, part, col = where_tile(tile)
        if found:
            at, b, p, c, w = found[-1]
            if (b, p, c + w) == (buf, part, col):
                found[-1] = (at, b, p, c, w + 128)
                continue
        found.append((128 * (tile - first), buf, part, col, 128))
    return found


def kernel(
    latent, mod, w_spatial, w_out, caption, w_text, w_cross, text_len, w_time, w_time_out, out,
    wsp, wa, wb, tx, nb, tok, res, s0, wqk, wvt, qb, kb, vt, scores, ot, oi,
    za, zb, ga, gb, gt, acc, xb, qt, at, ar, rs, rr, ssem, rsem,
):
    fr = lax.axis_index("frame")
    sp = lax.axis_index("space")
    y, xh = fr // 2, fr % 2
    xl, z, c = sp // 16, (sp // 2) % 8, sp % 2
    x = 2 * xh + xl
    oc = 1 - c

    def dev(y_, x_, z_, c_):
        return (y_ * 2 + x_ // 2, (x_ % 2) * 16 + z_ * 2 + c_)

    partner = dev(y, x, z, oc)
    zn = [dev(y, x, (z + 1) % 8, c), dev(y, x, (z + 7) % 8, c)]
    xn = [dev(y, (x + 1) % 4, z, c), dev(y, (x + 3) % 4, z, c)]
    xmate = dev(y, 2 * xh + (1 - xl), z, c)
    yn = [dev((y + d) % 4, x, z, c) for d in (1, 3)]

    ids = [0]
    started = []

    def reserve(n):
        first = ids[0]
        ids[0] += n
        return first

    def send(src, dst, target):
        i = reserve(1)
        copy = pltpu.make_async_remote_copy(
            src_ref=src, dst_ref=dst, send_sem=ssem.at[i], recv_sem=rsem.at[i],
            device_id=target, device_id_type=MESH,
        )
        copy.start()
        started.append(copy)
        return copy

    barrier = pltpu.get_barrier_semaphore()
    for i in range(1, 32):
        pl.semaphore_signal(barrier, inc=1, device_id=(fr, (sp + i) % 32), device_id_type=MESH)
    for i in range(1, 8):
        for core in range(2):
            pl.semaphore_signal(
                barrier, inc=1, device_id=((fr + i) % 8, xl * 16 + z * 2 + core), device_id_type=MESH
            )
    pl.semaphore_signal(
        barrier, inc=1, device_id=dev(y, 2 * (1 - xh) + (1 - xl), z, c), device_id_type=MESH
    )

    def tile_of(t):
        for ref, first in ((w_out, 0), (w_cross, 9), (w_time, 18), (w_time_out, 45)):
            if t - first < ref.shape[1] // 128:
                return ref[:, 128 * (t - first) : 128 * (t - first + 1)]
        return jnp.zeros((ROWS, 128), BF)

    for quarter in range(4):

        @pl.when(y == quarter)
        def _():
            for core in range(2):
                e = 2 * quarter + core
                for i, t in enumerate((2 * e, 2 * e + 1, 16 + e)):
                    wa[core, :, 128 * i : 128 * (i + 1)] = tile_of(t)
                for i in range(4):
                    wb[core, :, 128 * i : 128 * (i + 1)] = tile_of(24 + 4 * e + i)
            first = 2 * TROWS * quarter
            count = min(2 * TROWS, caption.shape[0] - first)
            text = nt(caption[first : first + count], w_text[...])
            text = jnp.concatenate([text, jnp.zeros((count, 128 - HD), F32)], axis=1)
            if count < 2 * TROWS:
                text = jnp.concatenate([text, jnp.zeros((2 * TROWS - count, 128), F32)], axis=0)
            tx[...] = text.astype(BF).reshape(2, TROWS, 128)

    part = 2 * y + c
    za[z, c] = wa[c]
    zb[z, c] = wb[c]
    gt[part, xl, z, c] = tx[c]

    for i in range(2):
        nb[i] = modulate(latent[i].astype(F32), mod[0:1], mod[1:2])
    tok[z, xl, c] = nb[xl]
    res[c] = latent[c]

    for h in range(HEADS):
        cols = [w_spatial[:, D * i + HD * h : D * i + HD * (h + 1)] for i in range(3)]
        wsp[h] = jnp.concatenate(cols + [jnp.zeros((ROWS, 256 - 3 * HD), BF)], axis=1)
    s0[xl, z, c] = wsp[2 * z + c]
    pl.semaphore_wait(barrier, 46)

    init_a = send(wa.at[oc], za.at[z, c], partner)
    init_t = send(tx.at[oc], gt.at[2 * y + oc, xl, z, c], partner)
    init_b = send(wb.at[oc], zb.at[z, c], partner)
    tok_x = send(nb.at[1 - xl], tok.at[z, xl, c], xmate)

    s_in = []

    def give_spatial(*offsets):
        for d in offsets:
            zt = (z + d) % 8
            if d:
                s_in.append(send(wsp.at[2 * zt + c], s0.at[xl, z, c], dev(y, x, zt, c)))
            s_in.append(send(wsp.at[2 * zt + oc], s0.at[xl, z, c], dev(y, x, zt, oc)))

    def block(step, way):
        return (z + (8 - step if way == 0 else step)) % 8

    class Ring:
        def __init__(self, whole, halves):
            self.whole, self.halves, self.copies = whole, halves, {}

        def go(self, step):
            for way in range(2):
                b = block(step, way)
                ref = self.whole(b) if step < 3 else self.halves(b, way)
                self.copies[step, way] = send(ref, ref, zn[way])

        def come(self, step):
            for way in range(2):
                self.copies[step - 1, way].wait_recv()

    ring_a = Ring(lambda b: za.at[b], lambda b, h: za.at[b, h])
    ring_b = Ring(lambda b: zb.at[b], lambda b, h: zb.at[b, h])
    ring_t = Ring(lambda b: gt.at[part, xl, b], lambda b, h: gt.at[part, xl, b, h])
    ring_0 = Ring(lambda b: tok.at[b, xl, c], None)
    ring_1 = Ring(lambda b: tok.at[b, 1 - xl, c], None)
    tok_core = {}

    def tok_ring(ring, sub, step):
        if step < 3:
            ring.go(step)
        else:
            b = block(3, 0 if sub == 0 else 1)
            way = 0 if sub == 0 else 1
            ref = tok.at[b, xl if sub == 0 else 1 - xl, c]
            ring.copies[3, way] = send(ref, ref, zn[way])

    def tok_share(b, lo, key):
        ref = tok.at[b, lo, c]
        tok_core[key] = send(ref, ref, partner)

    def tok_step(step):
        for way in range(2):
            for sub, ring in ((0, ring_0), (1, ring_1)):
                ring.copies[step - 1, way].wait_recv()
        if step < 4:
            tok_ring(ring_0, 0, step)
            tok_ring(ring_1, 1, step)
        for way in range(2):
            for sub in range(2):
                tok_share(block(step, way), xl if sub == 0 else 1 - xl, (step, way, sub))

    def tok_last():
        ring_0.copies[3, 0].wait_recv()
        ring_1.copies[3, 1].wait_recv()
        tok_share(block(4, 0), xl, (4, 0, 0))
        tok_share(block(4, 0), 1 - xl, (4, 0, 1))

    def tok_ready(step, way):
        for sub in range(2):
            tok_core[step, way, sub].wait_recv()

    class Spread:
        def __init__(self, lo_rows, half_rows):
            self.lo_rows, self.half_rows = lo_rows, half_rows
            self.x_copies, self.core_copies, self.y_halves = [], [], []

        def start(self):
            mine = self.lo_rows(part, xl)
            self.y_copies = [send(mine, mine, t) for t in yn]
            self.spread(y)

        def y_last(self):
            for copy in self.y_halves:
                copy.wait_recv()
            self.spread((y + 2) % 4)

        def spread(self, yq):
            e = 2 * yq + c
            xs = []
            for way in range(2):
                ref = self.half_rows(e, xl, way)
                xs.append(send(ref, ref, xn[way]))
            self.x_copies.append((e, xs))
            ref = self.lo_rows(e, xl)
            self.core_copies.append(send(ref, ref, partner))

        def y_come(self, k):
            self.y_copies[k].wait_recv()
            yq = (y + (3, 1)[k]) % 4
            ref = self.half_rows(2 * yq + c, xl, k)
            self.y_halves.append(send(ref, ref, yn[k]))
            self.spread(yq)

        def x_come(self, k):
            e, xs = self.x_copies[k]
            for way in range(2):
                xs[way].wait_recv()
                ref = self.half_rows(e, 1 - xl, way)
                self.core_copies.append(send(ref, ref, partner))

        def finish(self):
            for copy in self.core_copies:
                copy.wait_recv()

    def rows_of(buf):
        def lo_rows(e, lo):
            return buf.at[e, pl.ds(pl.multiple_of(lo * HALF, HALF), HALF)]

        def half_rows(e, lo, way):
            return buf.at[e, pl.ds(pl.multiple_of(lo * HALF + way * (HALF // 2), HALF // 2), HALF // 2)]

        return lo_rows, half_rows

    spread_a = Spread(*rows_of(ga))
    spread_b = Spread(*rows_of(gb))
    spread_t = Spread(
        lambda e, lo: gt.at[e, lo], lambda e, lo, way: gt.at[e, lo, pl.ds(4 * way, 4)]
    )

    def compact(zref, gref):
        for k in range(4):
            rows = jnp.concatenate([zref[2 * k + i // 2, i % 2] for i in range(4)], axis=0)
            gref[part, pl.ds(pl.multiple_of(xl * HALF + 144 * k, 144), 144)] = rows

    def qkv(b):
        rows = tok[b].reshape(256, D)
        qk = mm(rows, wqk[...]).astype(BF)
        qb[b] = qk[:, :128]
        kb[b] = qk[:, 128:]
        v = nt(wvt[...], rows)
        ones = lax.broadcasted_iota(jnp.int32, v.shape, 0) == HD
        vt[b] = jnp.where(ones, 1.0, v).astype(BF)

    rings = (ring_a, ring_t, ring_b)

    def weight_step(step):
        for ring in rings:
            ring.come(step)
            ring.go(step)

    for copy, ring in zip((init_a, init_t, init_b), rings):
        copy.wait_recv()
        ring.go(0)
    ring_0.go(0)
    tok_share(z, xl, (0, 0, 0))
    weight_step(1)
    tok_x.wait_recv()
    ring_1.go(0)
    tok_share(z, 1 - xl, (0, 0, 1))
    weight_step(2)
    weight_step(3)
    give_spatial(0, 1, 7, 2, 6, 3, 5, 4)
    ring_a.come(4)
    compact(za, ga)
    spread_a.start()
    ring_t.come(4)
    spread_t.start()
    ring_b.come(4)
    compact(zb, gb)
    spread_b.start()
    res_in = send(latent.at[oc], res.at[c], partner)
    tok_step(1)
    for copy in s_in:
        copy.wait_recv()
    s_x = [
        send(s0.at[xl, pl.ds(4 * way, 4)], s0.at[xl, pl.ds(4 * way, 4)], xn[way]) for way in range(2)
    ]
    tok_step(2)
    spread_a.y_come(0)
    spread_a.y_come(1)
    spread_a.x_come(0)
    spread_t.y_come(0)
    spread_t.y_come(1)
    spread_t.x_come(0)
    for copy in s_x:
        copy.wait_recv()
    joined = s0[...].reshape(32 * ROWS, 256).astype(F32)
    blank = jnp.zeros((D, 128 - HD), F32)
    wqk[...] = jnp.concatenate([joined[:, :HD], blank, joined[:, HD : 2 * HD], blank], axis=1).astype(BF)
    wvt[...] = jnp.concatenate([joined[:, 2 * HD : 3 * HD], blank], axis=1).T[:80].astype(BF)
    tok_ready(0, 0)
    qkv(z)
    for way in range(2):
        tok_ready(1, way)
        qkv(block(1, way))
    tok_step(3)
    for way in range(2):
        tok_ready(2, way)
        qkv(block(2, way))
    spread_a.y_last()
    spread_t.y_last()
    spread_b.x_come(0)
    tok_last()
    for way in range(2):
        tok_ready(3, way)
        qkv(block(3, way))
    tok_ready(4, 0)
    qkv(block(4, 0))
    spread_a.x_come(1)
    spread_a.x_come(2)
    spread_t.x_come(1)
    spread_t.x_come(2)

    oi_id = reserve(16)
    head = 2 * z + c

    def attn_copy(i, lo):
        zt = (z + 1 + i) % 8
        i_send = oi_id + 2 * i + lo
        return (
            pltpu.make_async_remote_copy(
                src_ref=ot.at[zt, lo], dst_ref=oi.at[head],
                send_sem=ssem.at[i_send], recv_sem=rsem.at[oi_id + head],
                device_id=(fr, lo * 16 + zt * 2 + xl), device_id_type=MESH,
            ),
            pltpu.make_async_copy(ot.at[zt, lo], oi.at[head], rsem.at[oi_id + head]),
            jnp.logical_and(zt == z, jnp.logical_and(xl == lo, c == xl)),
        )

    def tile(i, carry):
        zt = (z + 1 + i) % 8
        queries = qb[zt]
        top = jnp.full((1, 256), -jnp.inf, F32)
        for k in range(4):
            s = nt(kb[2 * k : 2 * k + 2].reshape(512, 128), queries)
            scores[512 * k : 512 * (k + 1)] = s
            top = jnp.maximum(top, jnp.max(s, axis=0, keepdims=True))
        top = top * (SCALE * LOG2E)
        total = jnp.zeros((80, 256), F32)
        for k in range(8):
            p = jnp.exp2(scores[256 * k : 256 * (k + 1)] * (SCALE * LOG2E) - top)
            total = total + mm(vt[k], p.astype(BF))
        mixed = (total[:HD] / total[HD : HD + 1]).astype(BF)
        for lo in range(2):
            ot[zt, lo] = mixed[:, 128 * lo : 128 * (lo + 1)]
            far, near, own = attn_copy(i, lo)

            @pl.when(own)
            def _():
                near.start()

            @pl.when(jnp.logical_not(own))
            def _():
                far.start()

        return carry

    lax.fori_loop(0, 2, tile, 0)
    spread_b.y_come(0)
    spread_b.y_come(1)
    lax.fori_loop(2, 5, tile, 0)
    spread_a.x_come(3)
    spread_t.x_come(3)
    lax.fori_loop(5, 8, tile, 0)
    spread_b.y_last()
    spread_b.x_come(1)
    for i in range(HEADS):
        pltpu.make_async_copy(ot.at[0, 0], oi.at[i], rsem.at[oi_id + i]).wait()

    bufs = (ga, gb)

    def project(rows, first, count, put):
        for at_col, buf, e, col, width in runs(first, count):
            put(at_col, width, mm(rows, bufs[buf][e, :, col : col + width]))

    def put_acc(at_col, width, value):
        acc[:, at_col : at_col + width] = value

    spread_a.finish()
    rows = oi[...].reshape(D, 128).T
    project(rows, 0, 9, put_acc)
    res_in.wait_recv()
    own = res[...].reshape(128, D).astype(F32)
    after_space = (own + mod[2:3] * acc[...]).astype(BF)

    def put_qt(at_col, width, value):
        qt[:, at_col : at_col + width] = value.astype(BF)

    project(after_space, 9, 9, put_qt)
    qt[:, D : D + 128] = jnp.zeros((128, 128), BF)
    spread_b.x_come(2)
    spread_t.finish()
    valid = lax.broadcasted_iota(jnp.int32, (128, TEXT), 1) < text_len[0]
    mixed = []
    for h in range(HEADS):
        keys = gt[:, 0, h // 2, h % 2].reshape(TEXT, 128)
        values = gt[:, 1, h // 2, h % 2].reshape(TEXT, 128)
        s = nt(qt[:, HD * h : HD * h + 128], keys) * SCALE
        s = jnp.where(valid, s, -jnp.inf)
        p = jnp.exp(s - jnp.max(s, axis=-1, keepdims=True))
        w = (p / jnp.sum(p, axis=-1, keepdims=True)).astype(BF)
        mixed.append(mm(w, values)[:, :HD])
    crossed = jnp.concatenate(mixed, axis=1).astype(BF)
    after_text = (after_space.astype(F32) + crossed.astype(F32)).astype(BF)
    at[...] = after_text.reshape(16, 8, D)

    me = 2 * fr + c
    ar[me] = at[me]
    time_in = []
    for k in range(1, 16):
        p = (me + k) % 16
        time_in.append(send(at.at[p], ar.at[me], (p // 2, xl * 16 + z * 2 + p % 2)))
    for copy in time_in:
        copy.wait_recv()
    tokens = ar[...].reshape(128, D).astype(F32)
    xb[...] = modulate(tokens, mod[3:4], mod[4:5])
    spread_b.x_come(3)
    spread_b.finish()
    project(xb[...], 18, 27, put_qt)
    qt[:, 3 * D :] = jnp.zeros((128, 128), BF)
    lanes = lax.broadcasted_iota(jnp.int32, (128, 128), 1)
    subs = lax.broadcasted_iota(jnp.int32, (128, 128), 0)
    same = (lanes % 8) == (subs % 8)
    real = lanes < HD
    mixed = []
    for h in range(HEADS):
        q = qt[:, HD * h : HD * h + 128]
        k = jnp.where(real, qt[:, D + HD * h : D + HD * h + 128], 0)
        v = qt[:, 2 * D + HD * h : 2 * D + HD * h + 128]
        s = jnp.where(same, nt(q, k) * SCALE, -jnp.inf)
        p = jnp.exp(s - jnp.max(s, axis=-1, keepdims=True))
        w = (p / jnp.sum(p, axis=-1, keepdims=True)).astype(BF)
        mixed.append(mm(w, v)[:, :HD])
    temporal = jnp.concatenate(mixed, axis=1).astype(BF)
    project(temporal, 45, 9, put_acc)
    result = (ar[...].reshape(128, D).astype(F32) + mod[5:6] * acc[...]).astype(BF)
    rs[...] = result.reshape(8, 2, 8, D)

    back_id = reserve(8)
    slot = (2 * fr + c) % 8
    back = []
    for k in range(8):
        ft = (fr + k) % 8
        far = pltpu.make_async_remote_copy(
            src_ref=rs.at[ft], dst_ref=rr.at[slot],
            send_sem=ssem.at[back_id + k], recv_sem=rsem.at[back_id + slot],
            device_id=(ft, xl * 16 + z * 2 + fr // 4), device_id_type=MESH,
        )
        back.append(far)
        if k == 0:
            near = pltpu.make_async_copy(rs.at[ft], rr.at[slot], rsem.at[back_id + slot])

            @pl.when(c == fr // 4)
            def _():
                near.start()

            @pl.when(c != fr // 4)
            def _():
                far.start()
        else:
            far.start()
    for k in range(8):
        pltpu.make_async_copy(rs.at[0], rr.at[k], rsem.at[back_id + k]).wait()
    for i in range(2):
        out[i] = rr[:, i].reshape(64, D)

    for copy in started:
        copy.wait_send()
    for i in range(8):
        for lo in range(2):
            far, near, own = attn_copy(i, lo)

            @pl.when(jnp.logical_not(own))
            def _():
                far.wait_send()

    @pl.when(c != fr // 4)
    def _():
        back[0].wait_send()

    for k in range(1, 8):
        back[k].wait_send()


def local(
    latent, modulation, w_spatial, w_spatial_out, caption_states, w_text_kv, w_cross_q, text_len,
    w_time, w_time_out,
):
    vmem = pl.BlockSpec(memory_space=pltpu.VMEM)
    return pl.pallas_call(
        kernel,
        out_shape=jax.ShapeDtypeStruct(latent.shape, BF),
        in_specs=[vmem] * 7 + [pl.BlockSpec(memory_space=pltpu.SMEM)] + [vmem] * 2,
        out_specs=vmem,
        scratch_shapes=[
            pltpu.VMEM((HEADS, ROWS, 256), BF),
            pltpu.VMEM((2, ROWS, CA), BF),
            pltpu.VMEM((2, ROWS, CB), BF),
            pltpu.VMEM((2, TROWS, 128), BF),
            pltpu.VMEM((2, 64, D), BF),
            pltpu.VMEM((8, 2, 2, 64, D), BF),
            pltpu.VMEM((2, 64, D), BF),
            pltpu.VMEM((2, 8, 2, ROWS, 256), BF),
            pltpu.VMEM((D, 256), BF),
            pltpu.VMEM((80, D), BF),
            pltpu.VMEM((8, 256, 128), BF),
            pltpu.VMEM((8, 256, 128), BF),
            pltpu.VMEM((8, 80, 256), BF),
            pltpu.VMEM((2048, 256), F32),
            pltpu.VMEM((8, 2, HD, 128), BF),
            pltpu.VMEM((HEADS, HD, 128), BF),
            pltpu.VMEM((8, 2, ROWS, CA), BF),
            pltpu.VMEM((8, 2, ROWS, CB), BF),
            pltpu.VMEM((8, D, CA), BF),
            pltpu.VMEM((8, D, CB), BF),
            pltpu.VMEM((8, 2, 8, 2, TROWS, 128), BF),
            pltpu.VMEM((128, D), F32),
            pltpu.VMEM((128, D), BF),
            pltpu.VMEM((128, 3 * D + 128), BF),
            pltpu.VMEM((16, 8, D), BF),
            pltpu.VMEM((16, 8, D), BF),
            pltpu.VMEM((8, 2, 8, D), BF),
            pltpu.VMEM((8, 2, 8, D), BF),
            pltpu.SemaphoreType.DMA((NSEM,)),
            pltpu.SemaphoreType.DMA((NSEM,)),
        ],
        compiler_params=pltpu.CompilerParams(
            collective_id=0, has_side_effects=True, vmem_limit_bytes=60 << 20
        ),
        name="block",
    )(
        latent, modulation, w_spatial, w_spatial_out, caption_states, w_text_kv.T, w_cross_q, text_len,
        w_time, w_time_out,
    )


def solution(mesh):
    placed = (
        P("frame", "space", None),
        P(),
        P("space", None),
        P("space", None),
        P(),
        P(None, "space"),
        P("space", None),
        P(),
        P("space", None),
        P("space", None),
    )
    return jax.shard_map(
        local, mesh=mesh, in_specs=placed, out_specs=P("frame", "space", None), check_vma=False
    )
```

```python
import functools
import math

import jax
import jax.numpy as jnp
from jax import lax
from jax.experimental import pallas as pl
from jax.experimental.pallas import tpu as pltpu
from jax.sharding import PartitionSpec as P

D = 1152
HEADS = 16
HD = 72
ROWS = 36
HALF = 576
TROWS = 40
TEXT = 8 * TROWS
CA = 384
CB = 384
CW = 768
MESH = pl.DeviceIdType.MESH
BF = jnp.bfloat16
F32 = jnp.float32
SCALE = 1.0 / math.sqrt(HD)
LOG2E = 1.4426950408889634
NSEM = 256


def modulate(values, shift, gain):
    row_mean = jnp.mean(values, axis=-1, keepdims=True)
    centred = values - row_mean
    variance = jnp.mean(centred * centred, axis=-1, keepdims=True)
    return (centred * lax.rsqrt(variance + 1e-06) * (1.0 + gain) + shift).astype(BF)


def nt(left, right):
    return lax.dot_general(left, right, (((1,), (1,)), ((), ())), preferred_element_type=F32)


def mm(left, right):
    return jnp.dot(left, right, preferred_element_type=F32)


def where_tile(tile):
    if tile < 16:
        return 0, tile // 2, 128 * (tile % 2)
    if tile < 24:
        return 0, tile - 16, 256
    if tile < 48:
        return 1, (tile - 24) // 3, 128 * (tile % 3)
    return 2, 0, 128 * (tile - 48)


def runs(first, count):
    found = []
    for tile in range(first, first + count):
        buf, part, col = where_tile(tile)
        if found:
            at, b, p, c, w = found[-1]
            if (b, p, c + w) == (buf, part, col):
                found[-1] = (at, b, p, c, w + 128)
                continue
        found.append((128 * (tile - first), buf, part, col, 128))
    return found


def kernel(
    latent, mod, w_spatial, w_out, caption, w_text, w_cross, text_len, w_time, w_time_out, out,
    wsp, wa, wb, tx, nb, tok, res, s0, wqk, wvt, qb, kb, vt, scores, ot, oi,
    za, zb, ga, gb, gt, w2, gw, acc, xb, qt, at, ar, rs, rr, ssem, rsem,
):
    fr = lax.axis_index("frame")
    sp = lax.axis_index("space")
    y, xh = fr // 2, fr % 2
    xl, z, c = sp // 16, (sp // 2) % 8, sp % 2
    x = 2 * xh + xl
    oc = 1 - c

    def dev(y_, x_, z_, c_):
        return (y_ * 2 + x_ // 2, (x_ % 2) * 16 + z_ * 2 + c_)

    partner = dev(y, x, z, oc)
    zn = [dev(y, x, (z + 1) % 8, c), dev(y, x, (z + 7) % 8, c)]
    xn = [dev(y, (x + 1) % 4, z, c), dev(y, (x + 3) % 4, z, c)]
    xmate = dev(y, 2 * xh + (1 - xl), z, c)
    yn = [dev((y + d) % 4, x, z, c) for d in (1, 3)]

    ids = [0]
    started = []

    def reserve(n):
        first = ids[0]
        ids[0] += n
        return first

    def send(src, dst, target):
        i = reserve(1)
        copy = pltpu.make_async_remote_copy(
            src_ref=src, dst_ref=dst, send_sem=ssem.at[i], recv_sem=rsem.at[i],
            device_id=target, device_id_type=MESH,
        )
        copy.start()
        started.append(copy)
        return copy

    barrier = pltpu.get_barrier_semaphore()
    for i in range(1, 32):
        pl.semaphore_signal(barrier, inc=1, device_id=(fr, (sp + i) % 32), device_id_type=MESH)
    for i in range(1, 8):
        for core in range(2):
            pl.semaphore_signal(
                barrier, inc=1, device_id=((fr + i) % 8, xl * 16 + z * 2 + core), device_id_type=MESH
            )
    pl.semaphore_signal(
        barrier, inc=1, device_id=dev(y, 2 * (1 - xh) + (1 - xl), z, c), device_id_type=MESH
    )

    def tile_of(t):
        for ref, first in ((w_out, 0), (w_cross, 9), (w_time, 18), (w_time_out, 45)):
            if t - first < ref.shape[1] // 128:
                return ref[:, 128 * (t - first) : 128 * (t - first + 1)]
        raise ValueError(t)

    for quarter in range(4):

        @pl.when(y == quarter)
        def _():
            for core in range(2):
                e = 2 * quarter + core
                for i, t in enumerate((2 * e, 2 * e + 1, 16 + e)):
                    wa[core, :, 128 * i : 128 * (i + 1)] = tile_of(t)
                for i in range(3):
                    wb[core, :, 128 * i : 128 * (i + 1)] = tile_of(24 + 3 * e + i)
            first = 2 * TROWS * quarter
            count = min(2 * TROWS, caption.shape[0] - first)
            text = nt(caption[first : first + count], w_text[...])
            text = jnp.concatenate([text, jnp.zeros((count, 128 - HD), F32)], axis=1)
            if count < 2 * TROWS:
                text = jnp.concatenate([text, jnp.zeros((2 * TROWS - count, 128), F32)], axis=0)
            tx[...] = text.astype(BF).reshape(2, TROWS, 128)

    part = 2 * y + c
    za[z, c] = wa[c]
    zb[z, c] = wb[c]
    gt[part, xl, z, c] = tx[c]

    for i in range(2):
        nb[i] = modulate(latent[i].astype(F32), mod[0:1], mod[1:2])
    tok[z, xl, c] = nb[xl]
    w2[z, xl, c] = w_time_out[:, 3 * 128 :]
    res[c] = latent[c]

    for h in range(HEADS):
        cols = [w_spatial[:, D * i + HD * h : D * i + HD * (h + 1)] for i in range(3)]
        wsp[h] = jnp.concatenate(cols + [jnp.zeros((ROWS, 256 - 3 * HD), BF)], axis=1)
    s0[xl, z, c] = wsp[2 * z + c]
    pl.semaphore_wait(barrier, 46)

    init_a = send(wa.at[oc], za.at[z, c], partner)
    init_t = send(tx.at[oc], gt.at[2 * y + oc, xl, z, c], partner)
    init_b = send(wb.at[oc], zb.at[z, c], partner)
    tok_x = send(nb.at[1 - xl], tok.at[z, xl, c], xmate)

    s_in = []

    def give_spatial(*offsets):
        for d in offsets:
            zt = (z + d) % 8
            if d:
                s_in.append(send(wsp.at[2 * zt + c], s0.at[xl, z, c], dev(y, x, zt, c)))
            s_in.append(send(wsp.at[2 * zt + oc], s0.at[xl, z, c], dev(y, x, zt, oc)))

    def block(step, way):
        return (z + (8 - step if way == 0 else step)) % 8

    class Ring:
        def __init__(self, whole, halves):
            self.whole, self.halves, self.copies = whole, halves, {}

        def go(self, step):
            for way in range(2):
                b = block(step, way)
                ref = self.whole(b) if step < 3 else self.halves(b, way)
                self.copies[step, way] = send(ref, ref, zn[way])

        def come(self, step):
            for way in range(2):
                self.copies[step - 1, way].wait_recv()

    ring_a = Ring(lambda b: za.at[b], lambda b, h: za.at[b, h])
    ring_b = Ring(lambda b: zb.at[b], lambda b, h: zb.at[b, h])
    ring_t = Ring(lambda b: gt.at[part, xl, b], lambda b, h: gt.at[part, xl, b, h])

    class Gather:
        def __init__(self, buf):
            self.buf, self.shared = buf, {}
            self.subs = (xl, 1 - xl)
            self.rings = [Ring(lambda b, lo=lo: buf.at[b, lo, c], None) for lo in self.subs]

        def go(self, sub, step):
            if step < 3:
                self.rings[sub].go(step)
            else:
                ref = self.buf.at[block(3, sub), self.subs[sub], c]
                self.rings[sub].copies[3, sub] = send(ref, ref, zn[sub])

        def share(self, step, way, sub):
            ref = self.buf.at[block(step, way), self.subs[sub], c]
            self.shared[step, way, sub] = send(ref, ref, partner)

        def first(self, sub):
            self.go(sub, 0)
            self.share(0, 0, sub)

        def step(self, step):
            for way in range(2):
                for ring in self.rings:
                    ring.copies[step - 1, way].wait_recv()
            for sub in range(2):
                self.go(sub, step)
            for way in range(2):
                for sub in range(2):
                    self.share(step, way, sub)

        def last(self):
            for sub in range(2):
                self.rings[sub].copies[3, sub].wait_recv()
            for sub in range(2):
                self.share(4, 0, sub)

        def ready(self, step, way):
            for sub in range(2):
                self.shared[step, way, sub].wait_recv()

    tokens_in = Gather(tok)
    wide_in = Gather(w2)

    class Spread:
        def __init__(self, lo_rows, half_rows):
            self.lo_rows, self.half_rows = lo_rows, half_rows
            self.x_copies, self.core_copies, self.y_halves = [], [], []

        def start(self):
            mine = self.lo_rows(part, xl)
            self.y_copies = [send(mine, mine, t) for t in yn]
            self.spread(y)

        def y_last(self):
            for copy in self.y_halves:
                copy.wait_recv()
            self.spread((y + 2) % 4)

        def spread(self, yq):
            e = 2 * yq + c
            xs = []
            for way in range(2):
                ref = self.half_rows(e, xl, way)
                xs.append(send(ref, ref, xn[way]))
            self.x_copies.append((e, xs))
            ref = self.lo_rows(e, xl)
            self.core_copies.append(send(ref, ref, partner))

        def y_come(self, k):
            self.y_copies[k].wait_recv()
            yq = (y + (3, 1)[k]) % 4
            ref = self.half_rows(2 * yq + c, xl, k)
            self.y_halves.append(send(ref, ref, yn[k]))
            self.spread(yq)

        def x_come(self, k):
            e, xs = self.x_copies[k]
            for way in range(2):
                xs[way].wait_recv()
                ref = self.half_rows(e, 1 - xl, way)
                self.core_copies.append(send(ref, ref, partner))

        def finish(self):
            for copy in self.core_copies:
                copy.wait_recv()

    def rows_of(buf):
        def lo_rows(e, lo):
            return buf.at[e, pl.ds(pl.multiple_of(lo * HALF, HALF), HALF)]

        def half_rows(e, lo, way):
            return buf.at[e, pl.ds(pl.multiple_of(lo * HALF + way * (HALF // 2), HALF // 2), HALF // 2)]

        return lo_rows, half_rows

    spread_a = Spread(*rows_of(ga))
    spread_b = Spread(*rows_of(gb))
    spread_t = Spread(
        lambda e, lo: gt.at[e, lo], lambda e, lo, way: gt.at[e, lo, pl.ds(4 * way, 4)]
    )

    def compact(zref, gref):
        for k in range(4):
            rows = jnp.concatenate([zref[2 * k + i // 2, i % 2] for i in range(4)], axis=0)
            gref[part, pl.ds(pl.multiple_of(xl * HALF + 144 * k, 144), 144)] = rows

    def qkv(b):
        rows = tok[b].reshape(256, D)
        qk = mm(rows, wqk[...]).astype(BF)
        qb[b] = qk[:, :128]
        kb[b] = qk[:, 128:]
        v = nt(wvt[...], rows)
        ones = lax.broadcasted_iota(jnp.int32, v.shape, 0) == HD
        vt[b] = jnp.where(ones, 1.0, v).astype(BF)

    rings = (ring_a, ring_t, ring_b)

    def weight_step(step):
        for ring in rings:
            ring.come(step)
            ring.go(step)

    for copy, ring in zip((init_a, init_t, init_b), rings):
        copy.wait_recv()
        ring.go(0)
    tokens_in.first(0)
    weight_step(1)
    tok_x.wait_recv()
    tokens_in.first(1)
    weight_step(2)
    weight_step(3)
    give_spatial(0, 1, 7, 2, 6, 3, 5, 4)
    ring_a.come(4)
    compact(za, ga)
    spread_a.start()
    ring_t.come(4)
    spread_t.start()
    ring_b.come(4)
    compact(zb, gb)
    spread_b.start()
    res_in = send(latent.at[oc], res.at[c], partner)
    tokens_in.step(1)
    for copy in s_in:
        copy.wait_recv()
    s_x = [
        send(s0.at[xl, pl.ds(4 * way, 4)], s0.at[xl, pl.ds(4 * way, 4)], xn[way]) for way in range(2)
    ]
    wide_x = send(w2.at[z, xl, c], w2.at[z, xl, c], xmate)
    tokens_in.step(2)
    spread_a.y_come(0)
    spread_a.y_come(1)
    spread_a.x_come(0)
    spread_t.y_come(0)
    spread_t.y_come(1)
    spread_t.x_come(0)
    for copy in s_x:
        copy.wait_recv()
    joined = s0[...].reshape(32 * ROWS, 256).astype(F32)
    blank = jnp.zeros((D, 128 - HD), F32)
    wqk[...] = jnp.concatenate([joined[:, :HD], blank, joined[:, HD : 2 * HD], blank], axis=1).astype(BF)
    wvt[...] = jnp.concatenate([joined[:, 2 * HD : 3 * HD], blank], axis=1).T[:80].astype(BF)
    tokens_in.ready(0, 0)
    qkv(z)
    for way in range(2):
        tokens_in.ready(1, way)
        qkv(block(1, way))
    tokens_in.step(3)
    for way in range(2):
        tokens_in.ready(2, way)
        qkv(block(2, way))
    spread_a.y_last()
    spread_t.y_last()
    spread_b.x_come(0)
    tokens_in.last()
    wide_in.first(0)
    wide_x.wait_recv()
    wide_in.first(1)
    for way in range(2):
        tokens_in.ready(3, way)
        qkv(block(3, way))
    tokens_in.ready(4, 0)
    qkv(block(4, 0))
    spread_a.x_come(1)
    spread_a.x_come(2)
    spread_t.x_come(1)
    spread_t.x_come(2)

    oi_id = reserve(16)
    head = 2 * z + c

    def attn_copy(i, lo):
        zt = (z + 1 + i) % 8
        i_send = oi_id + 2 * i + lo
        return (
            pltpu.make_async_remote_copy(
                src_ref=ot.at[zt, lo], dst_ref=oi.at[head],
                send_sem=ssem.at[i_send], recv_sem=rsem.at[oi_id + head],
                device_id=(fr, lo * 16 + zt * 2 + xl), device_id_type=MESH,
            ),
            pltpu.make_async_copy(ot.at[zt, lo], oi.at[head], rsem.at[oi_id + head]),
            jnp.logical_and(zt == z, jnp.logical_and(xl == lo, c == xl)),
        )

    def tile(i, carry):
        zt = (z + 1 + i) % 8
        queries = qb[zt]
        top = jnp.full((1, 256), -jnp.inf, F32)
        for k in range(4):
            s = nt(kb[2 * k : 2 * k + 2].reshape(512, 128), queries)
            scores[512 * k : 512 * (k + 1)] = s
            top = jnp.maximum(top, jnp.max(s, axis=0, keepdims=True))
        top = top * (SCALE * LOG2E)
        total = jnp.zeros((80, 256), F32)
        for k in range(8):
            p = jnp.exp2(scores[256 * k : 256 * (k + 1)] * (SCALE * LOG2E) - top)
            total = total + mm(vt[k], p.astype(BF))
        mixed = (total[:HD] / total[HD : HD + 1]).astype(BF)
        for lo in range(2):
            ot[zt, lo] = mixed[:, 128 * lo : 128 * (lo + 1)]
            far, near, own = attn_copy(i, lo)

            @pl.when(own)
            def _():
                near.start()

            @pl.when(jnp.logical_not(own))
            def _():
                far.start()

        return carry

    lax.fori_loop(0, 2, tile, 0)
    spread_b.y_come(0)
    spread_b.y_come(1)
    lax.fori_loop(2, 5, tile, 0)
    spread_a.x_come(3)
    spread_t.x_come(3)
    wide_in.step(1)
    lax.fori_loop(5, 8, tile, 0)
    spread_b.y_last()
    spread_b.x_come(1)
    wide_in.step(2)
    for i in range(HEADS):
        pltpu.make_async_copy(ot.at[0, 0], oi.at[i], rsem.at[oi_id + i]).wait()

    bufs = (ga, gb)

    def project(rows, first, count, put):
        for at_col, buf, e, col, width in runs(first, count):
            matrix = gw[:, col : col + width] if buf == 2 else bufs[buf][e, :, col : col + width]
            put(at_col, width, mm(rows, matrix))

    def put_acc(at_col, width, value):
        acc[:, at_col : at_col + width] = value

    spread_a.finish()
    rows = oi[...].reshape(D, 128).T
    project(rows, 0, 9, put_acc)
    res_in.wait_recv()
    own = res[...].reshape(128, D).astype(F32)
    after_space = (own + mod[2:3] * acc[...]).astype(BF)

    def put_qt(at_col, width, value):
        qt[:, at_col : at_col + width] = value.astype(BF)

    project(after_space, 9, 9, put_qt)
    qt[:, D : D + 128] = jnp.zeros((128, 128), BF)
    spread_b.x_come(2)
    wide_in.step(3)
    spread_t.finish()
    valid = lax.broadcasted_iota(jnp.int32, (128, TEXT), 1) < text_len[0]
    mixed = []
    for h in range(HEADS):
        keys = gt[:, 0, h // 2, h % 2].reshape(TEXT, 128)
        values = gt[:, 1, h // 2, h % 2].reshape(TEXT, 128)
        s = nt(qt[:, HD * h : HD * h + 128], keys) * SCALE
        s = jnp.where(valid, s, -jnp.inf)
        p = jnp.exp(s - jnp.max(s, axis=-1, keepdims=True))
        w = (p / jnp.sum(p, axis=-1, keepdims=True)).astype(BF)
        mixed.append(mm(w, values)[:, :HD])
    crossed = jnp.concatenate(mixed, axis=1).astype(BF)
    after_text = (after_space.astype(F32) + crossed.astype(F32)).astype(BF)
    at[...] = after_text.reshape(16, 8, D)

    wide_in.last()
    me = 2 * fr + c
    ar[me] = at[me]
    time_in = []
    for k in range(1, 16):
        p = (me + k) % 16
        time_in.append(send(at.at[p], ar.at[me], (p // 2, xl * 16 + z * 2 + p % 2)))
    for step, way in ((0, 0), (1, 0), (1, 1), (2, 0), (2, 1), (3, 0), (3, 1), (4, 0)):
        wide_in.ready(step, way)
    for lo in range(2):
        for k in range(4):
            rows = [w2[2 * k + i // 2, lo, i % 2] for i in range(4)]
            gw[HALF * lo + 144 * k : HALF * lo + 144 * (k + 1)] = jnp.concatenate(rows, axis=0)
    for copy in time_in:
        copy.wait_recv()
    tokens = ar[...].reshape(128, D).astype(F32)
    xb[...] = modulate(tokens, mod[3:4], mod[4:5])
    spread_b.x_come(3)
    spread_b.finish()
    project(xb[...], 18, 27, put_qt)
    qt[:, 3 * D :] = jnp.zeros((128, 128), BF)
    lanes = lax.broadcasted_iota(jnp.int32, (128, 128), 1)
    subs = lax.broadcasted_iota(jnp.int32, (128, 128), 0)
    same = (lanes % 8) == (subs % 8)
    real = lanes < HD
    mixed = []
    for h in range(HEADS):
        q = qt[:, HD * h : HD * h + 128]
        k = jnp.where(real, qt[:, D + HD * h : D + HD * h + 128], 0)
        v = qt[:, 2 * D + HD * h : 2 * D + HD * h + 128]
        s = jnp.where(same, nt(q, k) * SCALE, -jnp.inf)
        p = jnp.exp(s - jnp.max(s, axis=-1, keepdims=True))
        w = (p / jnp.sum(p, axis=-1, keepdims=True)).astype(BF)
        mixed.append(mm(w, v)[:, :HD])
    temporal = jnp.concatenate(mixed, axis=1).astype(BF)
    project(temporal, 45, 9, put_acc)
    result = (ar[...].reshape(128, D).astype(F32) + mod[5:6] * acc[...]).astype(BF)
    rs[...] = result.reshape(8, 2, 8, D)

    back_id = reserve(8)
    slot = (2 * fr + c) % 8
    back = []
    for k in range(8):
        ft = (fr + k) % 8
        far = pltpu.make_async_remote_copy(
            src_ref=rs.at[ft], dst_ref=rr.at[slot],
            send_sem=ssem.at[back_id + k], recv_sem=rsem.at[back_id + slot],
            device_id=(ft, xl * 16 + z * 2 + fr // 4), device_id_type=MESH,
        )
        back.append(far)
        if k == 0:
            near = pltpu.make_async_copy(rs.at[ft], rr.at[slot], rsem.at[back_id + slot])

            @pl.when(c == fr // 4)
            def _():
                near.start()

            @pl.when(c != fr // 4)
            def _():
                far.start()
        else:
            far.start()
    for k in range(8):
        pltpu.make_async_copy(rs.at[0], rr.at[k], rsem.at[back_id + k]).wait()
    for i in range(2):
        out[i] = rr[:, i].reshape(64, D)

    for copy in started:
        copy.wait_send()
    for i in range(8):
        for lo in range(2):
            far, near, own = attn_copy(i, lo)

            @pl.when(jnp.logical_not(own))
            def _():
                far.wait_send()

    @pl.when(c != fr // 4)
    def _():
        back[0].wait_send()

    for k in range(1, 8):
        back[k].wait_send()


def local(
    latent, modulation, w_spatial, w_spatial_out, caption_states, w_text_kv, w_cross_q, text_len,
    w_time, w_time_out,
):
    vmem = pl.BlockSpec(memory_space=pltpu.VMEM)
    return pl.pallas_call(
        kernel,
        out_shape=jax.ShapeDtypeStruct(latent.shape, BF),
        in_specs=[vmem] * 7 + [pl.BlockSpec(memory_space=pltpu.SMEM)] + [vmem] * 2,
        out_specs=vmem,
        scratch_shapes=[
            pltpu.VMEM((HEADS, ROWS, 256), BF),
            pltpu.VMEM((2, ROWS, CA), BF),
            pltpu.VMEM((2, ROWS, CB), BF),
            pltpu.VMEM((2, TROWS, 128), BF),
            pltpu.VMEM((2, 64, D), BF),
            pltpu.VMEM((8, 2, 2, 64, D), BF),
            pltpu.VMEM((2, 64, D), BF),
            pltpu.VMEM((2, 8, 2, ROWS, 256), BF),
            pltpu.VMEM((D, 256), BF),
            pltpu.VMEM((80, D), BF),
            pltpu.VMEM((8, 256, 128), BF),
            pltpu.VMEM((8, 256, 128), BF),
            pltpu.VMEM((8, 80, 256), BF),
            pltpu.VMEM((2048, 256), F32),
            pltpu.VMEM((8, 2, HD, 128), BF),
            pltpu.VMEM((HEADS, HD, 128), BF),
            pltpu.VMEM((8, 2, ROWS, CA), BF),
            pltpu.VMEM((8, 2, ROWS, CB), BF),
            pltpu.VMEM((8, D, CA), BF),
            pltpu.VMEM((8, D, CB), BF),
            pltpu.VMEM((8, 2, 8, 2, TROWS, 128), BF),
            pltpu.VMEM((8, 2, 2, ROWS, CW), BF),
            pltpu.VMEM((D, CW), BF),
            pltpu.VMEM((128, D), F32),
            pltpu.VMEM((128, D), BF),
            pltpu.VMEM((128, 3 * D + 128), BF),
            pltpu.VMEM((16, 8, D), BF),
            pltpu.VMEM((16, 8, D), BF),
            pltpu.VMEM((8, 2, 8, D), BF),
            pltpu.VMEM((8, 2, 8, D), BF),
            pltpu.SemaphoreType.DMA((NSEM,)),
            pltpu.SemaphoreType.DMA((NSEM,)),
        ],
        compiler_params=pltpu.CompilerParams(
            collective_id=0, has_side_effects=True, vmem_limit_bytes=60 << 20
        ),
        name="block",
    )(
        latent, modulation, w_spatial, w_spatial_out, caption_states, w_text_kv.T, w_cross_q, text_len,
        w_time, w_time_out,
    )


def solution(mesh):
    placed = (
        P("frame", "space", None),
        P(),
        P("space", None),
        P("space", None),
        P(),
        P(None, "space"),
        P("space", None),
        P(),
        P("space", None),
        P("space", None),
    )
    return jax.shard_map(
        local, mesh=mesh, in_specs=placed, out_specs=P("frame", "space", None), check_vma=False
    )
```

```python
import functools
import math

import jax
import jax.numpy as jnp
from jax import lax
from jax.experimental import pallas as pl
from jax.experimental.pallas import tpu as pltpu
from jax.sharding import PartitionSpec as P

D = 1152
HEADS = 16
HD = 72
ROWS = 36
HALF = 576
TROWS = 40
TEXT = 8 * TROWS
CA = 384
CB = 384
CW = 768
MESH = pl.DeviceIdType.MESH
BF = jnp.bfloat16
F32 = jnp.float32
SCALE = 1.0 / math.sqrt(HD)
LOG2E = 1.4426950408889634
NSEM = 256


def modulate(values, shift, gain):
    row_mean = jnp.mean(values, axis=-1, keepdims=True)
    centred = values - row_mean
    variance = jnp.mean(centred * centred, axis=-1, keepdims=True)
    return (centred * lax.rsqrt(variance + 1e-06) * (1.0 + gain) + shift).astype(BF)


def nt(left, right):
    return lax.dot_general(left, right, (((1,), (1,)), ((), ())), preferred_element_type=F32)


def mm(left, right):
    return jnp.dot(left, right, preferred_element_type=F32)


def where_tile(tile):
    if tile < 16:
        return 0, tile // 2, 128 * (tile % 2)
    if tile < 24:
        return 0, tile - 16, 256
    if tile < 48:
        return 1, (tile - 24) // 3, 128 * (tile % 3)
    return 2, 0, 128 * (tile - 48)


def runs(first, count):
    found = []
    for tile in range(first, first + count):
        buf, part, col = where_tile(tile)
        if found:
            at, b, p, c, w = found[-1]
            if (b, p, c + w) == (buf, part, col):
                found[-1] = (at, b, p, c, w + 128)
                continue
        found.append((128 * (tile - first), buf, part, col, 128))
    return found


def kernel(
    latent, mod, w_spatial, w_out, caption, w_text, w_cross, text_len, w_time, w_time_out, out,
    wsp, wa, wb, tx, nb, tok, res, s0, wqk, wvt, qb, kb, vt, scores, ot, oi,
    za, zb, ga, gb, gt, w2, gw, acc, xb, qt, at, ar, rs, rr, ssem, rsem,
):
    fr = lax.axis_index("frame")
    sp = lax.axis_index("space")
    y, xh = fr // 2, fr % 2
    xl, z, c = sp // 16, (sp // 2) % 8, sp % 2
    x = 2 * xh + xl
    oc = 1 - c

    def dev(y_, x_, z_, c_):
        return (y_ * 2 + x_ // 2, (x_ % 2) * 16 + z_ * 2 + c_)

    partner = dev(y, x, z, oc)
    zn = [dev(y, x, (z + 1) % 8, c), dev(y, x, (z + 7) % 8, c)]
    xn = [dev(y, (x + 1) % 4, z, c), dev(y, (x + 3) % 4, z, c)]
    xmate = dev(y, 2 * xh + (1 - xl), z, c)
    yn = [dev((y + d) % 4, x, z, c) for d in (1, 3)]

    ids = [0]
    started = []

    def reserve(n):
        first = ids[0]
        ids[0] += n
        return first

    def send(src, dst, target):
        i = reserve(1)
        copy = pltpu.make_async_remote_copy(
            src_ref=src, dst_ref=dst, send_sem=ssem.at[i], recv_sem=rsem.at[i],
            device_id=target, device_id_type=MESH,
        )
        copy.start()
        started.append(copy)
        return copy

    barrier = pltpu.get_barrier_semaphore()
    for i in range(1, 32):
        pl.semaphore_signal(barrier, inc=1, device_id=(fr, (sp + i) % 32), device_id_type=MESH)
    for i in range(1, 8):
        for core in range(2):
            pl.semaphore_signal(
                barrier, inc=1, device_id=((fr + i) % 8, xl * 16 + z * 2 + core), device_id_type=MESH
            )
    pl.semaphore_signal(
        barrier, inc=1, device_id=dev(y, 2 * (1 - xh) + (1 - xl), z, c), device_id_type=MESH
    )

    def tile_of(t):
        for ref, first in ((w_out, 0), (w_cross, 9), (w_time, 18), (w_time_out, 45)):
            if t - first < ref.shape[1] // 128:
                return ref[:, 128 * (t - first) : 128 * (t - first + 1)]
        raise ValueError(t)

    for quarter in range(4):

        @pl.when(y == quarter)
        def _():
            for core in range(2):
                e = 2 * quarter + core
                for i, t in enumerate((2 * e, 2 * e + 1, 16 + e)):
                    wa[core, :, 128 * i : 128 * (i + 1)] = tile_of(t)
                for i in range(3):
                    wb[core, :, 128 * i : 128 * (i + 1)] = tile_of(24 + 3 * e + i)
            first = 2 * TROWS * quarter
            count = min(2 * TROWS, caption.shape[0] - first)
            text = nt(caption[first : first + count], w_text[...])
            text = jnp.concatenate([text, jnp.zeros((count, 128 - HD), F32)], axis=1)
            if count < 2 * TROWS:
                text = jnp.concatenate([text, jnp.zeros((2 * TROWS - count, 128), F32)], axis=0)
            tx[...] = text.astype(BF).reshape(2, TROWS, 128)

    part = 2 * y + c
    za[z, c] = wa[c]
    zb[z, c] = wb[c]
    gt[part, xl, z, c] = tx[c]

    for i in range(2):
        nb[i] = modulate(latent[i].astype(F32), mod[0:1], mod[1:2])
    tok[z, xl, c] = nb[xl]
    w2[z, xl, c] = w_time_out[:, 3 * 128 :]
    res[c] = latent[c]

    for h in range(HEADS):
        cols = [w_spatial[:, D * i + HD * h : D * i + HD * (h + 1)] for i in range(3)]
        wsp[h] = jnp.concatenate(cols + [jnp.zeros((ROWS, 256 - 3 * HD), BF)], axis=1)
    s0[xl, z, c] = wsp[2 * z + c]
    pl.semaphore_wait(barrier, 46)

    init_a = send(wa.at[oc], za.at[z, c], partner)
    init_t = send(tx.at[oc], gt.at[2 * y + oc, xl, z, c], partner)
    init_b = send(wb.at[oc], zb.at[z, c], partner)
    tok_x = send(nb.at[1 - xl], tok.at[z, xl, c], xmate)

    s_in = []

    def give_spatial(*offsets):
        for d in offsets:
            zt = (z + d) % 8
            if d:
                s_in.append(send(wsp.at[2 * zt + c], s0.at[xl, z, c], dev(y, x, zt, c)))
            s_in.append(send(wsp.at[2 * zt + oc], s0.at[xl, z, c], dev(y, x, zt, oc)))

    def block(step, way):
        return (z + (8 - step if way == 0 else step)) % 8

    class Ring:
        def __init__(self, whole, halves):
            self.whole, self.halves, self.copies = whole, halves, {}

        def go(self, step):
            for way in range(2):
                b = block(step, way)
                ref = self.whole(b) if step < 3 else self.halves(b, way)
                self.copies[step, way] = send(ref, ref, zn[way])

        def come(self, step):
            for way in range(2):
                self.copies[step - 1, way].wait_recv()

    ring_a = Ring(lambda b: za.at[b], lambda b, h: za.at[b, h])
    ring_b = Ring(lambda b: zb.at[b], lambda b, h: zb.at[b, h])
    ring_t = Ring(lambda b: gt.at[part, xl, b], lambda b, h: gt.at[part, xl, b, h])

    class Gather:
        def __init__(self, buf):
            self.buf, self.shared = buf, {}
            self.subs = (xl, 1 - xl)
            self.rings = [Ring(lambda b, lo=lo: buf.at[b, lo, c], None) for lo in self.subs]

        def go(self, sub, step):
            if step < 3:
                self.rings[sub].go(step)
            else:
                ref = self.buf.at[block(3, sub), self.subs[sub], c]
                self.rings[sub].copies[3, sub] = send(ref, ref, zn[sub])

        def share(self, step, way, sub):
            ref = self.buf.at[block(step, way), self.subs[sub], c]
            self.shared[step, way, sub] = send(ref, ref, partner)

        def first(self, sub):
            self.go(sub, 0)
            self.share(0, 0, sub)

        def step(self, step):
            for way in range(2):
                for ring in self.rings:
                    ring.copies[step - 1, way].wait_recv()
            for sub in range(2):
                self.go(sub, step)
            for way in range(2):
                for sub in range(2):
                    self.share(step, way, sub)

        def last(self):
            for sub in range(2):
                self.rings[sub].copies[3, sub].wait_recv()
            for sub in range(2):
                self.share(4, 0, sub)

        def ready(self, step, way):
            for sub in range(2):
                self.shared[step, way, sub].wait_recv()

    tokens_in = Gather(tok)
    wide_in = Gather(w2)

    class Spread:
        def __init__(self, lo_rows, half_rows):
            self.lo_rows, self.half_rows = lo_rows, half_rows
            self.x_copies, self.core_copies, self.y_halves = [], [], []

        def start(self):
            mine = self.lo_rows(part, xl)
            self.y_copies = [send(mine, mine, t) for t in yn]
            self.spread(y)

        def y_last(self):
            for copy in self.y_halves:
                copy.wait_recv()
            self.spread((y + 2) % 4)

        def spread(self, yq):
            e = 2 * yq + c
            xs = []
            for way in range(2):
                ref = self.half_rows(e, xl, way)
                xs.append(send(ref, ref, xn[way]))
            self.x_copies.append((e, xs))
            ref = self.lo_rows(e, xl)
            self.core_copies.append(send(ref, ref, partner))

        def y_come(self, k):
            self.y_copies[k].wait_recv()
            yq = (y + (3, 1)[k]) % 4
            ref = self.half_rows(2 * yq + c, xl, k)
            self.y_halves.append(send(ref, ref, yn[k]))
            self.spread(yq)

        def x_come(self, k):
            e, xs = self.x_copies[k]
            for way in range(2):
                xs[way].wait_recv()
                ref = self.half_rows(e, 1 - xl, way)
                self.core_copies.append(send(ref, ref, partner))

        def finish(self):
            for copy in self.core_copies:
                copy.wait_recv()

    def rows_of(buf):
        def lo_rows(e, lo):
            return buf.at[e, pl.ds(pl.multiple_of(lo * HALF, HALF), HALF)]

        def half_rows(e, lo, way):
            return buf.at[e, pl.ds(pl.multiple_of(lo * HALF + way * (HALF // 2), HALF // 2), HALF // 2)]

        return lo_rows, half_rows

    spread_a = Spread(*rows_of(ga))
    spread_b = Spread(*rows_of(gb))
    spread_t = Spread(
        lambda e, lo: gt.at[e, lo], lambda e, lo, way: gt.at[e, lo, pl.ds(4 * way, 4)]
    )

    def compact(zref, gref):
        for k in range(4):
            rows = jnp.concatenate([zref[2 * k + i // 2, i % 2] for i in range(4)], axis=0)
            gref[part, pl.ds(pl.multiple_of(xl * HALF + 144 * k, 144), 144)] = rows

    def qkv(b):
        rows = tok[b].reshape(256, D)
        qk = mm(rows, wqk[...]).astype(BF)
        qb[b] = qk[:, :128]
        kb[b] = qk[:, 128:]
        v = nt(wvt[...], rows)
        ones = lax.broadcasted_iota(jnp.int32, v.shape, 0) == HD
        vt[b] = jnp.where(ones, 1.0, v).astype(BF)

    rings = (ring_a, ring_t, ring_b)

    def weight_step(step):
        for ring in rings:
            ring.come(step)
            ring.go(step)

    for copy, ring in zip((init_a, init_t, init_b), rings):
        copy.wait_recv()
        ring.go(0)
    tokens_in.first(0)
    weight_step(1)
    tok_x.wait_recv()
    tokens_in.first(1)
    weight_step(2)
    weight_step(3)
    give_spatial(0, 1, 7, 2, 6, 3, 5, 4)
    ring_a.come(4)
    compact(za, ga)
    spread_a.start()
    ring_t.come(4)
    spread_t.start()
    ring_b.come(4)
    compact(zb, gb)
    spread_b.start()
    res_in = send(latent.at[oc], res.at[c], partner)
    tokens_in.step(1)
    for copy in s_in:
        copy.wait_recv()
    s_x = [
        send(s0.at[xl, pl.ds(4 * way, 4)], s0.at[xl, pl.ds(4 * way, 4)], xn[way]) for way in range(2)
    ]
    wide_x = send(w2.at[z, xl, c], w2.at[z, xl, c], xmate)
    tokens_in.step(2)
    spread_a.y_come(0)
    spread_a.y_come(1)
    spread_a.x_come(0)
    spread_t.y_come(0)
    spread_t.y_come(1)
    spread_t.x_come(0)
    for copy in s_x:
        copy.wait_recv()
    joined = s0[...].reshape(32 * ROWS, 256).astype(F32)
    blank = jnp.zeros((D, 128 - HD), F32)
    wqk[...] = jnp.concatenate([joined[:, :HD], blank, joined[:, HD : 2 * HD], blank], axis=1).astype(BF)
    wvt[...] = jnp.concatenate([joined[:, 2 * HD : 3 * HD], blank], axis=1).T[:80].astype(BF)
    tokens_in.ready(0, 0)
    qkv(z)
    for way in range(2):
        tokens_in.ready(1, way)
        qkv(block(1, way))
    tokens_in.step(3)
    for way in range(2):
        tokens_in.ready(2, way)
        qkv(block(2, way))
    spread_a.y_last()
    spread_t.y_last()
    spread_b.x_come(0)
    tokens_in.last()
    wide_in.first(0)
    wide_x.wait_recv()
    wide_in.first(1)
    for way in range(2):
        tokens_in.ready(3, way)
        qkv(block(3, way))
    tokens_in.ready(4, 0)
    qkv(block(4, 0))
    spread_a.x_come(1)
    spread_a.x_come(2)
    spread_t.x_come(1)
    spread_t.x_come(2)

    oi_id = reserve(16)
    head = 2 * z + c

    def attn_copy(i, lo):
        zt = (z + 1 + i) % 8
        i_send = oi_id + 2 * i + lo
        return (
            pltpu.make_async_remote_copy(
                src_ref=ot.at[zt, lo], dst_ref=oi.at[head],
                send_sem=ssem.at[i_send], recv_sem=rsem.at[oi_id + head],
                device_id=(fr, lo * 16 + zt * 2 + xl), device_id_type=MESH,
            ),
            pltpu.make_async_copy(ot.at[zt, lo], oi.at[head], rsem.at[oi_id + head]),
            jnp.logical_and(zt == z, jnp.logical_and(xl == lo, c == xl)),
        )

    def tile(i, carry):
        zt = (z + 1 + i) % 8
        queries = qb[zt]
        top = jnp.full((1, 256), -jnp.inf, F32)
        for k in range(4):
            s = nt(kb[2 * k : 2 * k + 2].reshape(512, 128), queries)
            scores[512 * k : 512 * (k + 1)] = s
            top = jnp.maximum(top, jnp.max(s, axis=0, keepdims=True))
        top = top * (SCALE * LOG2E)
        total = jnp.zeros((80, 256), F32)
        for k in range(8):
            p = jnp.exp2(scores[256 * k : 256 * (k + 1)] * (SCALE * LOG2E) - top)
            total = total + mm(vt[k], p.astype(BF))
        mixed = (total[:HD] / total[HD : HD + 1]).astype(BF)
        for lo in range(2):
            ot[zt, lo] = mixed[:, 128 * lo : 128 * (lo + 1)]
            far, near, own = attn_copy(i, lo)

            @pl.when(own)
            def _():
                near.start()

            @pl.when(jnp.logical_not(own))
            def _():
                far.start()

        return carry

    lax.fori_loop(0, 2, tile, 0)
    spread_b.y_come(0)
    spread_b.y_come(1)
    lax.fori_loop(2, 5, tile, 0)
    spread_a.x_come(3)
    spread_t.x_come(3)
    wide_in.step(1)
    lax.fori_loop(5, 8, tile, 0)
    spread_b.y_last()
    spread_b.x_come(1)
    wide_in.step(2)
    for i in range(HEADS):
        pltpu.make_async_copy(ot.at[0, 0], oi.at[i], rsem.at[oi_id + i]).wait()

    bufs = (ga, gb)

    def project(rows, first, count, put):
        for at_col, buf, e, col, width in runs(first, count):
            matrix = gw[:, col : col + width] if buf == 2 else bufs[buf][e, :, col : col + width]
            put(at_col, width, mm(rows, matrix))

    def put_acc(at_col, width, value):
        acc[:, at_col : at_col + width] = value

    spread_a.finish()
    rows = oi[...].reshape(D, 128).T
    project(rows, 0, 9, put_acc)
    res_in.wait_recv()
    own = res[...].reshape(128, D).astype(F32)
    after_space = (own + mod[2:3] * acc[...]).astype(BF)

    def put_qt(at_col, width, value):
        qt[:, at_col : at_col + width] = value.astype(BF)

    project(after_space, 9, 9, put_qt)
    qt[:, D : D + 128] = jnp.zeros((128, 128), BF)
    spread_b.x_come(2)
    wide_in.step(3)
    spread_t.finish()
    valid = lax.broadcasted_iota(jnp.int32, (128, TEXT), 1) < text_len[0]
    mixed = []
    ones = jnp.ones((TEXT, 128), BF)
    for h in range(HEADS):
        keys = gt[:, 0, h // 2, h % 2].reshape(TEXT, 128)
        values = gt[:, 1, h // 2, h % 2].reshape(TEXT, 128)
        s = nt(qt[:, HD * h : HD * h + 128], keys) * (SCALE * LOG2E)
        s = jnp.where(valid, s, -jnp.inf)
        p = jnp.exp2(s - jnp.max(s, axis=-1, keepdims=True)).astype(BF)
        both = mm(p, jnp.concatenate([values, ones], axis=1))
        mixed.append((both[:, :128] / both[:, 128:])[:, :HD])
    crossed = jnp.concatenate(mixed, axis=1).astype(BF)
    after_text = (after_space.astype(F32) + crossed.astype(F32)).astype(BF)
    at[...] = after_text.reshape(16, 8, D)

    wide_in.last()
    me = 2 * fr + c
    ar[me] = at[me]
    time_in = []
    for k in range(1, 16):
        p = (me + k) % 16
        time_in.append(send(at.at[p], ar.at[me], (p // 2, xl * 16 + z * 2 + p % 2)))
    for step, way in ((0, 0), (1, 0), (1, 1), (2, 0), (2, 1), (3, 0), (3, 1), (4, 0)):
        wide_in.ready(step, way)
    for lo in range(2):
        for k in range(4):
            rows = [w2[2 * k + i // 2, lo, i % 2] for i in range(4)]
            gw[HALF * lo + 144 * k : HALF * lo + 144 * (k + 1)] = jnp.concatenate(rows, axis=0)
    for copy in time_in:
        copy.wait_recv()
    tokens = ar[...].reshape(128, D).astype(F32)
    xb[...] = modulate(tokens, mod[3:4], mod[4:5])
    spread_b.x_come(3)
    spread_b.finish()
    project(xb[...], 18, 27, put_qt)
    lanes = lax.broadcasted_iota(jnp.int32, (128, 256), 1)
    subs = lax.broadcasted_iota(jnp.int32, (128, 256), 0)
    same = ((lanes % 8) == (subs % 8))[:, :128]
    ones = jnp.ones((128, 256), BF)
    tiles = [[] for _ in range(D // 128)]
    for h in range(HEADS):
        first = HD * h // 128
        width = 128 * ((HD * h + HD - 1) // 128 - first + 1)
        base = 128 * first
        own = jnp.logical_and(lanes >= HD * h - base, lanes < HD * (h + 1) - base)[:, :width]
        q = qt[:, base : base + width]
        k = jnp.where(own, qt[:, D + base : D + base + width], 0)
        v = jnp.where(own, qt[:, 2 * D + base : 2 * D + base + width], 0)
        s = jnp.where(same, nt(q, k) * (SCALE * LOG2E), -jnp.inf)
        p = jnp.exp2(s - jnp.max(s, axis=-1, keepdims=True)).astype(BF)
        o = mm(p, v) / mm(p, ones[:, :width])
        for i in range(width // 128):
            tiles[first + i].append(o[:, 128 * i : 128 * (i + 1)])
    temporal = jnp.concatenate([sum(t) for t in tiles], axis=1).astype(BF)
    project(temporal, 45, 9, put_acc)
    result = (ar[...].reshape(128, D).astype(F32) + mod[5:6] * acc[...]).astype(BF)
    rs[...] = result.reshape(8, 2, 8, D)

    back_id = reserve(8)
    slot = (2 * fr + c) % 8
    back = []
    for k in range(8):
        ft = (fr + k) % 8
        far = pltpu.make_async_remote_copy(
            src_ref=rs.at[ft], dst_ref=rr.at[slot],
            send_sem=ssem.at[back_id + k], recv_sem=rsem.at[back_id + slot],
            device_id=(ft, xl * 16 + z * 2 + fr // 4), device_id_type=MESH,
        )
        back.append(far)
        if k == 0:
            near = pltpu.make_async_copy(rs.at[ft], rr.at[slot], rsem.at[back_id + slot])

            @pl.when(c == fr // 4)
            def _():
                near.start()

            @pl.when(c != fr // 4)
            def _():
                far.start()
        else:
            far.start()
    for k in range(8):
        pltpu.make_async_copy(rs.at[0], rr.at[k], rsem.at[back_id + k]).wait()
    for i in range(2):
        out[i] = rr[:, i].reshape(64, D)

    for copy in started:
        copy.wait_send()
    for i in range(8):
        for lo in range(2):
            far, near, own = attn_copy(i, lo)

            @pl.when(jnp.logical_not(own))
            def _():
                far.wait_send()

    @pl.when(c != fr // 4)
    def _():
        back[0].wait_send()

    for k in range(1, 8):
        back[k].wait_send()


def local(
    latent, modulation, w_spatial, w_spatial_out, caption_states, w_text_kv, w_cross_q, text_len,
    w_time, w_time_out,
):
    vmem = pl.BlockSpec(memory_space=pltpu.VMEM)
    return pl.pallas_call(
        kernel,
        out_shape=jax.ShapeDtypeStruct(latent.shape, BF),
        in_specs=[vmem] * 7 + [pl.BlockSpec(memory_space=pltpu.SMEM)] + [vmem] * 2,
        out_specs=vmem,
        scratch_shapes=[
            pltpu.VMEM((HEADS, ROWS, 256), BF),
            pltpu.VMEM((2, ROWS, CA), BF),
            pltpu.VMEM((2, ROWS, CB), BF),
            pltpu.VMEM((2, TROWS, 128), BF),
            pltpu.VMEM((2, 64, D), BF),
            pltpu.VMEM((8, 2, 2, 64, D), BF),
            pltpu.VMEM((2, 64, D), BF),
            pltpu.VMEM((2, 8, 2, ROWS, 256), BF),
            pltpu.VMEM((D, 256), BF),
            pltpu.VMEM((80, D), BF),
            pltpu.VMEM((8, 256, 128), BF),
            pltpu.VMEM((8, 256, 128), BF),
            pltpu.VMEM((8, 80, 256), BF),
            pltpu.VMEM((2048, 256), F32),
            pltpu.VMEM((8, 2, HD, 128), BF),
            pltpu.VMEM((HEADS, HD, 128), BF),
            pltpu.VMEM((8, 2, ROWS, CA), BF),
            pltpu.VMEM((8, 2, ROWS, CB), BF),
            pltpu.VMEM((8, D, CA), BF),
            pltpu.VMEM((8, D, CB), BF),
            pltpu.VMEM((8, 2, 8, 2, TROWS, 128), BF),
            pltpu.VMEM((8, 2, 2, ROWS, CW), BF),
            pltpu.VMEM((D, CW), BF),
            pltpu.VMEM((128, D), F32),
            pltpu.VMEM((128, D), BF),
            pltpu.VMEM((128, 3 * D + 128), BF),
            pltpu.VMEM((16, 8, D), BF),
            pltpu.VMEM((16, 8, D), BF),
            pltpu.VMEM((8, 2, 8, D), BF),
            pltpu.VMEM((8, 2, 8, D), BF),
            pltpu.SemaphoreType.DMA((NSEM,)),
            pltpu.SemaphoreType.DMA((NSEM,)),
        ],
        compiler_params=pltpu.CompilerParams(
            collective_id=0, has_side_effects=True, vmem_limit_bytes=60 << 20
        ),
        name="block",
    )(
        latent, modulation, w_spatial, w_spatial_out, caption_states, w_text_kv.T, w_cross_q, text_len,
        w_time, w_time_out,
    )


def solution(mesh):
    placed = (
        P("frame", "space", None),
        P(),
        P("space", None),
        P("space", None),
        P(),
        P(None, "space"),
        P("space", None),
        P(),
        P("space", None),
        P("space", None),
    )
    return jax.shard_map(
        local, mesh=mesh, in_specs=placed, out_specs=P("frame", "space", None), check_vma=False
    )
```

```python
import functools
import math

import jax
import jax.numpy as jnp
from jax import lax
from jax.experimental import pallas as pl
from jax.experimental.pallas import tpu as pltpu
from jax.sharding import PartitionSpec as P

D = 1152
HEADS = 16
HD = 72
ROWS = 36
HALF = 576
TROWS = 40
TEXT = 8 * TROWS
CA = 384
CB = 384
CW = 768
MESH = pl.DeviceIdType.MESH
BF = jnp.bfloat16
F32 = jnp.float32
SCALE = 1.0 / math.sqrt(HD)
LOG2E = 1.4426950408889634
NSEM = 256


def modulate(values, shift, gain):
    row_mean = jnp.mean(values, axis=-1, keepdims=True)
    centred = values - row_mean
    variance = jnp.mean(centred * centred, axis=-1, keepdims=True)
    return (centred * lax.rsqrt(variance + 1e-06) * (1.0 + gain) + shift).astype(BF)


def nt(left, right):
    return lax.dot_general(left, right, (((1,), (1,)), ((), ())), preferred_element_type=F32)


def mm(left, right):
    return jnp.dot(left, right, preferred_element_type=F32)


def where_tile(tile):
    if tile < 16:
        return 0, tile // 2, 128 * (tile % 2)
    if tile < 24:
        return 0, tile - 16, 256
    if tile < 48:
        return 1, (tile - 24) // 3, 128 * (tile % 3)
    return 2, 0, 128 * (tile - 48)


def runs(first, count):
    found = []
    for tile in range(first, first + count):
        buf, part, col = where_tile(tile)
        if found:
            at, b, p, c, w = found[-1]
            if (b, p, c + w) == (buf, part, col):
                found[-1] = (at, b, p, c, w + 128)
                continue
        found.append((128 * (tile - first), buf, part, col, 128))
    return found


def kernel(
    latent, mod, w_spatial, w_out, caption, w_text, w_cross, text_len, w_time, w_time_out, out,
    wsp, wa, wb, tx, nb, tok, res, s0, wqk, wvt, qb, kb, vt, scores, odd, ot, oi,
    za, zb, ga, gb, gt, w2, gw, acc, xb, qt, at, ar, rs, rr, ssem, rsem,
):
    fr = lax.axis_index("frame")
    sp = lax.axis_index("space")
    y, xh = fr // 2, fr % 2
    xl, z, c = sp // 16, (sp // 2) % 8, sp % 2
    x = 2 * xh + xl
    oc = 1 - c

    def dev(y_, x_, z_, c_):
        return (y_ * 2 + x_ // 2, (x_ % 2) * 16 + z_ * 2 + c_)

    partner = dev(y, x, z, oc)
    zn = [dev(y, x, (z + 1) % 8, c), dev(y, x, (z + 7) % 8, c)]
    xn = [dev(y, (x + 1) % 4, z, c), dev(y, (x + 3) % 4, z, c)]
    xmate = dev(y, 2 * xh + (1 - xl), z, c)
    yn = [dev((y + d) % 4, x, z, c) for d in (1, 3)]

    ids = [0]
    started = []

    def reserve(n):
        first = ids[0]
        ids[0] += n
        return first

    def send(src, dst, target):
        i = reserve(1)
        copy = pltpu.make_async_remote_copy(
            src_ref=src, dst_ref=dst, send_sem=ssem.at[i], recv_sem=rsem.at[i],
            device_id=target, device_id_type=MESH,
        )
        copy.start()
        started.append(copy)
        return copy

    barrier = pltpu.get_barrier_semaphore()
    for i in range(1, 32):
        pl.semaphore_signal(barrier, inc=1, device_id=(fr, (sp + i) % 32), device_id_type=MESH)
    for i in range(1, 8):
        for core in range(2):
            pl.semaphore_signal(
                barrier, inc=1, device_id=((fr + i) % 8, xl * 16 + z * 2 + core), device_id_type=MESH
            )
    pl.semaphore_signal(
        barrier, inc=1, device_id=dev(y, 2 * (1 - xh) + (1 - xl), z, c), device_id_type=MESH
    )

    def tile_of(t):
        for ref, first in ((w_out, 0), (w_cross, 9), (w_time, 18), (w_time_out, 45)):
            if t - first < ref.shape[1] // 128:
                return ref[:, 128 * (t - first) : 128 * (t - first + 1)]
        raise ValueError(t)

    for quarter in range(4):

        @pl.when(y == quarter)
        def _():
            for core in range(2):
                e = 2 * quarter + core
                for i, t in enumerate((2 * e, 2 * e + 1, 16 + e)):
                    wa[core, :, 128 * i : 128 * (i + 1)] = tile_of(t)
                for i in range(3):
                    wb[core, :, 128 * i : 128 * (i + 1)] = tile_of(24 + 3 * e + i)
            first = 2 * TROWS * quarter
            count = min(2 * TROWS, caption.shape[0] - first)
            text = nt(caption[first : first + count], w_text[...])
            text = jnp.concatenate([text, jnp.zeros((count, 128 - HD), F32)], axis=1)
            if count < 2 * TROWS:
                text = jnp.concatenate([text, jnp.zeros((2 * TROWS - count, 128), F32)], axis=0)
            tx[...] = text.astype(BF).reshape(2, TROWS, 128)

    part = 2 * y + c
    za[z, c] = wa[c]
    zb[z, c] = wb[c]
    gt[part, xl, z, c] = tx[c]

    for i in range(2):
        nb[i] = modulate(latent[i].astype(F32), mod[0:1], mod[1:2])
    tok[z, xl, c] = nb[xl]
    w2[z, xl, c] = w_time_out[:, 3 * 128 :]
    res[c] = latent[c]

    for h in range(HEADS):
        cols = [w_spatial[:, D * i + HD * h : D * i + HD * (h + 1)] for i in range(3)]
        wsp[h] = jnp.concatenate(cols + [jnp.zeros((ROWS, 256 - 3 * HD), BF)], axis=1)
    s0[xl, z, c] = wsp[2 * z + c]
    pl.semaphore_wait(barrier, 46)

    init_a = send(wa.at[oc], za.at[z, c], partner)
    init_t = send(tx.at[oc], gt.at[2 * y + oc, xl, z, c], partner)
    init_b = send(wb.at[oc], zb.at[z, c], partner)
    tok_x = send(nb.at[1 - xl], tok.at[z, xl, c], xmate)

    s_in = []

    def give_spatial(*offsets):
        for d in offsets:
            zt = (z + d) % 8
            if d:
                s_in.append(send(wsp.at[2 * zt + c], s0.at[xl, z, c], dev(y, x, zt, c)))
            s_in.append(send(wsp.at[2 * zt + oc], s0.at[xl, z, c], dev(y, x, zt, oc)))

    def block(step, way):
        return (z + (8 - step if way == 0 else step)) % 8

    class Ring:
        def __init__(self, whole, halves):
            self.whole, self.halves, self.copies = whole, halves, {}

        def go(self, step):
            for way in range(2):
                b = block(step, way)
                ref = self.whole(b) if step < 3 else self.halves(b, way)
                self.copies[step, way] = send(ref, ref, zn[way])

        def come(self, step):
            for way in range(2):
                self.copies[step - 1, way].wait_recv()

    ring_a = Ring(lambda b: za.at[b], lambda b, h: za.at[b, h])
    ring_b = Ring(lambda b: zb.at[b], lambda b, h: zb.at[b, h])
    ring_t = Ring(lambda b: gt.at[part, xl, b], lambda b, h: gt.at[part, xl, b, h])

    class Gather:
        def __init__(self, buf):
            self.buf, self.shared = buf, {}
            self.subs = (xl, 1 - xl)
            self.rings = [Ring(lambda b, lo=lo: buf.at[b, lo, c], None) for lo in self.subs]

        def go(self, sub, step):
            if step < 3:
                self.rings[sub].go(step)
            else:
                ref = self.buf.at[block(3, sub), self.subs[sub], c]
                self.rings[sub].copies[3, sub] = send(ref, ref, zn[sub])

        def share(self, step, way, sub):
            ref = self.buf.at[block(step, way), self.subs[sub], c]
            self.shared[step, way, sub] = send(ref, ref, partner)

        def first(self, sub):
            self.go(sub, 0)
            self.share(0, 0, sub)

        def step(self, step):
            for way in range(2):
                for ring in self.rings:
                    ring.copies[step - 1, way].wait_recv()
            for sub in range(2):
                self.go(sub, step)
            for way in range(2):
                for sub in range(2):
                    self.share(step, way, sub)

        def last(self):
            for sub in range(2):
                self.rings[sub].copies[3, sub].wait_recv()
            for sub in range(2):
                self.share(4, 0, sub)

        def ready(self, step, way):
            for sub in range(2):
                self.shared[step, way, sub].wait_recv()

    tokens_in = Gather(tok)
    wide_in = Gather(w2)

    class Spread:
        def __init__(self, lo_rows, half_rows):
            self.lo_rows, self.half_rows = lo_rows, half_rows
            self.x_copies, self.core_copies, self.y_halves = [], [], []

        def start(self):
            mine = self.lo_rows(part, xl)
            self.y_copies = [send(mine, mine, t) for t in yn]
            self.spread(y)

        def y_last(self):
            for copy in self.y_halves:
                copy.wait_recv()
            self.spread((y + 2) % 4)

        def spread(self, yq):
            e = 2 * yq + c
            xs = []
            for way in range(2):
                ref = self.half_rows(e, xl, way)
                xs.append(send(ref, ref, xn[way]))
            self.x_copies.append((e, xs))
            ref = self.lo_rows(e, xl)
            self.core_copies.append(send(ref, ref, partner))

        def y_come(self, k):
            self.y_copies[k].wait_recv()
            yq = (y + (3, 1)[k]) % 4
            ref = self.half_rows(2 * yq + c, xl, k)
            self.y_halves.append(send(ref, ref, yn[k]))
            self.spread(yq)

        def x_come(self, k):
            e, xs = self.x_copies[k]
            for way in range(2):
                xs[way].wait_recv()
                ref = self.half_rows(e, 1 - xl, way)
                self.core_copies.append(send(ref, ref, partner))

        def finish(self):
            for copy in self.core_copies:
                copy.wait_recv()

    def rows_of(buf):
        def lo_rows(e, lo):
            return buf.at[e, pl.ds(pl.multiple_of(lo * HALF, HALF), HALF)]

        def half_rows(e, lo, way):
            return buf.at[e, pl.ds(pl.multiple_of(lo * HALF + way * (HALF // 2), HALF // 2), HALF // 2)]

        return lo_rows, half_rows

    spread_a = Spread(*rows_of(ga))
    spread_b = Spread(*rows_of(gb))
    spread_t = Spread(
        lambda e, lo: gt.at[e, lo], lambda e, lo, way: gt.at[e, lo, pl.ds(4 * way, 4)]
    )

    def compact(zref, gref):
        for k in range(4):
            rows = jnp.concatenate([zref[2 * k + i // 2, i % 2] for i in range(4)], axis=0)
            gref[part, pl.ds(pl.multiple_of(xl * HALF + 144 * k, 144), 144)] = rows

    def qkv(b):
        rows = tok[b].reshape(256, D)
        qk = mm(rows, wqk[...]).astype(BF)
        qb[b] = qk[:, :128]
        kb[b] = qk[:, 128:]
        v = nt(wvt[...], rows)
        ones = lax.broadcasted_iota(jnp.int32, v.shape, 0) == HD
        vt[b] = jnp.where(ones, 1.0, v).astype(BF)

    rings = (ring_a, ring_t, ring_b)

    def weight_step(step):
        for ring in rings:
            ring.come(step)
            ring.go(step)

    for copy, ring in zip((init_a, init_t, init_b), rings):
        copy.wait_recv()
        ring.go(0)
    tokens_in.first(0)
    weight_step(1)
    tok_x.wait_recv()
    tokens_in.first(1)
    weight_step(2)
    weight_step(3)
    give_spatial(0, 1, 7, 2, 6, 3, 5, 4)
    ring_a.come(4)
    compact(za, ga)
    spread_a.start()
    ring_t.come(4)
    spread_t.start()
    ring_b.come(4)
    compact(zb, gb)
    spread_b.start()
    res_in = send(latent.at[oc], res.at[c], partner)
    tokens_in.step(1)
    for copy in s_in:
        copy.wait_recv()
    s_x = [
        send(s0.at[xl, pl.ds(4 * way, 4)], s0.at[xl, pl.ds(4 * way, 4)], xn[way]) for way in range(2)
    ]
    wide_x = send(w2.at[z, xl, c], w2.at[z, xl, c], xmate)
    tokens_in.step(2)
    spread_a.y_come(0)
    spread_a.y_come(1)
    spread_a.x_come(0)
    spread_t.y_come(0)
    spread_t.y_come(1)
    spread_t.x_come(0)
    for copy in s_x:
        copy.wait_recv()
    joined = s0[...].reshape(32 * ROWS, 256).astype(F32)
    blank = jnp.zeros((D, 128 - HD), F32)
    wqk[...] = jnp.concatenate([joined[:, :HD], blank, joined[:, HD : 2 * HD], blank], axis=1).astype(BF)
    wvt[...] = jnp.concatenate([joined[:, 2 * HD : 3 * HD], blank], axis=1).T[:80].astype(BF)
    tokens_in.ready(0, 0)
    qkv(z)
    for way in range(2):
        tokens_in.ready(1, way)
        qkv(block(1, way))
    tokens_in.step(3)
    for way in range(2):
        tokens_in.ready(2, way)
        qkv(block(2, way))
    spread_a.y_last()
    spread_t.y_last()
    spread_b.x_come(0)
    tokens_in.last()
    wide_in.first(0)
    wide_x.wait_recv()
    wide_in.first(1)
    for way in range(2):
        tokens_in.ready(3, way)
        qkv(block(3, way))
    tokens_in.ready(4, 0)
    qkv(block(4, 0))
    spread_a.x_come(1)
    spread_a.x_come(2)
    spread_t.x_come(1)
    spread_t.x_come(2)

    oi_id = reserve(16)
    head = 2 * z + c

    def attn_copy(i, lo):
        zt = (z + 1 + i) % 8
        i_send = oi_id + 2 * i + lo
        return (
            pltpu.make_async_remote_copy(
                src_ref=ot.at[zt, lo], dst_ref=oi.at[head],
                send_sem=ssem.at[i_send], recv_sem=rsem.at[oi_id + head],
                device_id=(fr, lo * 16 + zt * 2 + xl), device_id_type=MESH,
            ),
            pltpu.make_async_copy(ot.at[zt, lo], oi.at[head], rsem.at[oi_id + head]),
            jnp.logical_and(zt == z, jnp.logical_and(xl == lo, c == xl)),
        )

    fold = SCALE * LOG2E

    def score(buf, k, queries, top):
        s = nt(kb[2 * k : 2 * k + 2].reshape(512, 128), queries)
        buf[512 * k : 512 * (k + 1)] = s
        return jnp.maximum(top, jnp.max(s, axis=0, keepdims=True))

    nothing = jnp.full((1, 256), -jnp.inf, F32)

    def tile(i, now, later, top):
        zt = (z + 1 + i) % 8
        queries = qb[(z + 2 + i) % 8]
        above = nothing
        top = top * fold
        total = jnp.zeros((80, 256), F32)
        for k in range(4):
            if later is not None:
                above = score(later, k, queries, above)
            for j in (2 * k, 2 * k + 1):
                p = jnp.exp2(now[256 * j : 256 * (j + 1)] * fold - top)
                total = total + mm(vt[j], p.astype(BF))
        mixed = (total[:HD] / total[HD : HD + 1]).astype(BF)
        for lo in range(2):
            ot[zt, lo] = mixed[:, 128 * lo : 128 * (lo + 1)]
            far, near, own = attn_copy(i, lo)

            @pl.when(own)
            def _():
                near.start()

            @pl.when(jnp.logical_not(own))
            def _():
                far.start()

        return above

    def pair(i, top):
        return tile(2 * i + 1, odd, scores, tile(2 * i, scores, odd, top))

    top = nothing
    for k in range(4):
        top = score(scores, k, qb[(z + 1) % 8], top)
    top = lax.fori_loop(0, 1, pair, top)
    spread_b.y_come(0)
    spread_b.y_come(1)
    top = lax.fori_loop(1, 2, pair, top)
    spread_a.x_come(3)
    spread_t.x_come(3)
    wide_in.step(1)
    top = lax.fori_loop(2, 3, pair, top)
    tile(7, odd, None, tile(6, scores, odd, top))
    spread_b.y_last()
    spread_b.x_come(1)
    wide_in.step(2)
    for i in range(HEADS):
        pltpu.make_async_copy(ot.at[0, 0], oi.at[i], rsem.at[oi_id + i]).wait()

    bufs = (ga, gb)

    def project(rows, first, count, put):
        for at_col, buf, e, col, width in runs(first, count):
            matrix = gw[:, col : col + width] if buf == 2 else bufs[buf][e, :, col : col + width]
            put(at_col, width, mm(rows, matrix))

    def put_acc(at_col, width, value):
        acc[:, at_col : at_col + width] = value

    spread_a.finish()
    rows = oi[...].reshape(D, 128).T
    project(rows, 0, 9, put_acc)
    res_in.wait_recv()
    own = res[...].reshape(128, D).astype(F32)
    after_space = (own + mod[2:3] * acc[...]).astype(BF)

    def put_qt(at_col, width, value):
        qt[:, at_col : at_col + width] = value.astype(BF)

    project(after_space, 9, 9, put_qt)
    qt[:, D : D + 128] = jnp.zeros((128, 128), BF)
    spread_b.x_come(2)
    wide_in.step(3)
    spread_t.finish()
    valid = lax.broadcasted_iota(jnp.int32, (128, TEXT), 1) < text_len[0]
    mixed = []
    ones = jnp.ones((TEXT, 128), BF)
    for h in range(HEADS):
        keys = gt[:, 0, h // 2, h % 2].reshape(TEXT, 128)
        values = gt[:, 1, h // 2, h % 2].reshape(TEXT, 128)
        s = nt(qt[:, HD * h : HD * h + 128], keys) * (SCALE * LOG2E)
        s = jnp.where(valid, s, -jnp.inf)
        p = jnp.exp2(s - jnp.max(s, axis=-1, keepdims=True)).astype(BF)
        both = mm(p, jnp.concatenate([values, ones], axis=1))
        mixed.append((both[:, :128] / both[:, 128:])[:, :HD])
    crossed = jnp.concatenate(mixed, axis=1).astype(BF)
    after_text = (after_space.astype(F32) + crossed.astype(F32)).astype(BF)
    at[...] = after_text.reshape(16, 8, D)

    wide_in.last()
    me = 2 * fr + c
    ar[me] = at[me]
    time_in = []
    for k in range(1, 16):
        p = (me + k) % 16
        time_in.append(send(at.at[p], ar.at[me], (p // 2, xl * 16 + z * 2 + p % 2)))
    for step, way in ((0, 0), (1, 0), (1, 1), (2, 0), (2, 1), (3, 0), (3, 1), (4, 0)):
        wide_in.ready(step, way)
    for lo in range(2):
        for k in range(4):
            rows = [w2[2 * k + i // 2, lo, i % 2] for i in range(4)]
            gw[HALF * lo + 144 * k : HALF * lo + 144 * (k + 1)] = jnp.concatenate(rows, axis=0)
    for copy in time_in:
        copy.wait_recv()
    tokens = ar[...].reshape(128, D).astype(F32)
    xb[...] = modulate(tokens, mod[3:4], mod[4:5])
    spread_b.x_come(3)
    spread_b.finish()
    project(xb[...], 18, 27, put_qt)
    lanes = lax.broadcasted_iota(jnp.int32, (128, 256), 1)
    subs = lax.broadcasted_iota(jnp.int32, (128, 256), 0)
    same = ((lanes % 8) == (subs % 8))[:, :128]
    ones = jnp.ones((128, 256), BF)
    tiles = [[] for _ in range(D // 128)]
    for h in range(HEADS):
        first = HD * h // 128
        width = 128 * ((HD * h + HD - 1) // 128 - first + 1)
        base = 128 * first
        own = jnp.logical_and(lanes >= HD * h - base, lanes < HD * (h + 1) - base)[:, :width]
        q = qt[:, base : base + width]
        k = jnp.where(own, qt[:, D + base : D + base + width], 0)
        v = jnp.where(own, qt[:, 2 * D + base : 2 * D + base + width], 0)
        s = jnp.where(same, nt(q, k) * (SCALE * LOG2E), -jnp.inf)
        p = jnp.exp2(s - jnp.max(s, axis=-1, keepdims=True)).astype(BF)
        o = mm(p, v) / mm(p, ones[:, :width])
        for i in range(width // 128):
            tiles[first + i].append(o[:, 128 * i : 128 * (i + 1)])
    temporal = jnp.concatenate([sum(t) for t in tiles], axis=1).astype(BF)
    project(temporal, 45, 9, put_acc)
    result = (ar[...].reshape(128, D).astype(F32) + mod[5:6] * acc[...]).astype(BF)
    rs[...] = result.reshape(8, 2, 8, D)

    back_id = reserve(8)
    slot = (2 * fr + c) % 8
    back = []
    for k in range(8):
        ft = (fr + k) % 8
        far = pltpu.make_async_remote_copy(
            src_ref=rs.at[ft], dst_ref=rr.at[slot],
            send_sem=ssem.at[back_id + k], recv_sem=rsem.at[back_id + slot],
            device_id=(ft, xl * 16 + z * 2 + fr // 4), device_id_type=MESH,
        )
        back.append(far)
        if k == 0:
            near = pltpu.make_async_copy(rs.at[ft], rr.at[slot], rsem.at[back_id + slot])

            @pl.when(c == fr // 4)
            def _():
                near.start()

            @pl.when(c != fr // 4)
            def _():
                far.start()
        else:
            far.start()
    for k in range(8):
        pltpu.make_async_copy(rs.at[0], rr.at[k], rsem.at[back_id + k]).wait()
    for i in range(2):
        out[i] = rr[:, i].reshape(64, D)

    for copy in started:
        copy.wait_send()
    for i in range(8):
        for lo in range(2):
            far, near, own = attn_copy(i, lo)

            @pl.when(jnp.logical_not(own))
            def _():
                far.wait_send()

    @pl.when(c != fr // 4)
    def _():
        back[0].wait_send()

    for k in range(1, 8):
        back[k].wait_send()


def local(
    latent, modulation, w_spatial, w_spatial_out, caption_states, w_text_kv, w_cross_q, text_len,
    w_time, w_time_out,
):
    vmem = pl.BlockSpec(memory_space=pltpu.VMEM)
    return pl.pallas_call(
        kernel,
        out_shape=jax.ShapeDtypeStruct(latent.shape, BF),
        in_specs=[vmem] * 7 + [pl.BlockSpec(memory_space=pltpu.SMEM)] + [vmem] * 2,
        out_specs=vmem,
        scratch_shapes=[
            pltpu.VMEM((HEADS, ROWS, 256), BF),
            pltpu.VMEM((2, ROWS, CA), BF),
            pltpu.VMEM((2, ROWS, CB), BF),
            pltpu.VMEM((2, TROWS, 128), BF),
            pltpu.VMEM((2, 64, D), BF),
            pltpu.VMEM((8, 2, 2, 64, D), BF),
            pltpu.VMEM((2, 64, D), BF),
            pltpu.VMEM((2, 8, 2, ROWS, 256), BF),
            pltpu.VMEM((D, 256), BF),
            pltpu.VMEM((80, D), BF),
            pltpu.VMEM((8, 256, 128), BF),
            pltpu.VMEM((8, 256, 128), BF),
            pltpu.VMEM((8, 80, 256), BF),
            pltpu.VMEM((2048, 256), F32),
            pltpu.VMEM((2048, 256), F32),
            pltpu.VMEM((8, 2, HD, 128), BF),
            pltpu.VMEM((HEADS, HD, 128), BF),
            pltpu.VMEM((8, 2, ROWS, CA), BF),
            pltpu.VMEM((8, 2, ROWS, CB), BF),
            pltpu.VMEM((8, D, CA), BF),
            pltpu.VMEM((8, D, CB), BF),
            pltpu.VMEM((8, 2, 8, 2, TROWS, 128), BF),
            pltpu.VMEM((8, 2, 2, ROWS, CW), BF),
            pltpu.VMEM((D, CW), BF),
            pltpu.VMEM((128, D), F32),
            pltpu.VMEM((128, D), BF),
            pltpu.VMEM((128, 3 * D + 128), BF),
            pltpu.VMEM((16, 8, D), BF),
            pltpu.VMEM((16, 8, D), BF),
            pltpu.VMEM((8, 2, 8, D), BF),
            pltpu.VMEM((8, 2, 8, D), BF),
            pltpu.SemaphoreType.DMA((NSEM,)),
            pltpu.SemaphoreType.DMA((NSEM,)),
        ],
        compiler_params=pltpu.CompilerParams(
            collective_id=0, has_side_effects=True, vmem_limit_bytes=60 << 20
        ),
        name="block",
    )(
        latent, modulation, w_spatial, w_spatial_out, caption_states, w_text_kv.T, w_cross_q, text_len,
        w_time, w_time_out,
    )


def solution(mesh):
    placed = (
        P("frame", "space", None),
        P(),
        P("space", None),
        P("space", None),
        P(),
        P(None, "space"),
        P("space", None),
        P(),
        P("space", None),
        P("space", None),
    )
    return jax.shard_map(
        local, mesh=mesh, in_specs=placed, out_specs=P("frame", "space", None), check_vma=False
    )
```
